256 devices in a mesh: rep: 16 (over z_hi, x), table: 16 (over z_lo, y, core).
Axes of the slice: x: 4, y: 4, z: 8 (z_hi: 4, z_lo: 2; z = z_hi * 2 + z_lo), core: 2. Of those that a mesh axis runs over, the one named last changes fastest.
Arguments:
- dense_out: bfloat16 [32768, 128], P(('rep', 'table')), may hold values from -6 to 6
- pooled: bfloat16 [32768, 2048], P(('rep', 'table')), may hold values from -6 to 6
- cotangent: bfloat16 [32768, 2176], P(('rep', 'table')), may hold values from -24 to 24
- proj_v: bfloat16 [2176, 384], replicated, may hold values from -0.125 to 0.125
- proj_u: bfloat16 [384, 2176], replicated, may hold values from -0.3125 to 0.3125
- bias: float32 [2176], replicated, may hold values from -3 to 3
- lookup_slot: int32 [32768, 16, 2], P('rep', 'table'), may hold values from 0 to 2047, as said below
- uniq_rows: int32 [16, 16, 2048], P('rep', 'table'), may hold values from 0 to 8191, as said below
Outputs:
- grad_u: float32 [384, 2176], P('rep', 'table')
- grad_v: float32 [2176, 384], P('table', 'rep')
- grad_bias: float32 [2176], replicated
- row_grad: float32 [16, 8192, 128], P('table', 'rep')
The draws below stay inside these ranges and needn't reach their ends.
Inputs may be any that keep to these rules, and one draw needn't show every extreme that they name: `lookup_slot`: within one replica group and table, every place 0 to 2047 of the distinct-row list is named by at least one lookup. `uniq_rows`: the 2048 rows listed for one replica group and table are distinct; at most 160 of them lie in one block of rows r * 512 to (r + 1) * 512 - 1, and some block holds exactly 160.
All inputs are finite; a program needn't handle non-finite values.
Results may differ from the reference program's by a relative error of at most 0.007.
Values may be sent and summed in bfloat16 or wider, within the bound.
No kernel may reach another device: no remote copies, remote signals or barrier semaphores. Data moves between devices by JAX's collectives and lax.ppermute only.
A program may use at most 64 MiB of HBM per device.

```python
import jax
import jax.numpy as jnp
from jax import lax

EMB = 128
R = 384
POOL = 2
B_DEV = 128
ROWS_DEV = 512
TABLES = 16
D0 = 2176
SAMPLES = 32768
ROWS = 8192
UNIQ = 2048
N_REP = 16
N_TABLE = 16


def draw_lookup_slot(key, part):
    key = jax.random.fold_in(key, 11)
    lookups = B_DEV * N_TABLE * POOL
    key_list = jax.random.split(key, N_REP * TABLES)

    def draw_pair(subkey):
        key_a, key_b, key_c, key_d = jax.random.split(subkey, 4)
        covering = jax.random.permutation(key_a, UNIQ).astype(jnp.int32)
        low_pick = jax.random.randint(key_b, (lookups - UNIQ,), 0, UNIQ)
        second = jax.random.randint(key_c, (lookups - UNIQ,), 0, UNIQ)
        rest_ids = jnp.minimum(low_pick, second).astype(jnp.int32)
        slot_ids = jnp.concatenate([covering, rest_ids])
        return jax.random.permutation(key_d, slot_ids)
    slot_ids = jax.vmap(draw_pair)(key_list).reshape(N_REP, TABLES, B_DEV * N_TABLE, POOL)
    return jnp.transpose(slot_ids, (0, 2, 1, 3)).reshape(N_REP * B_DEV * N_TABLE, TABLES, POOL).astype(jnp.int32)


def draw_uniq_rows(key, part):
    key = jax.random.fold_in(key, 23)
    key_list = jax.random.split(key, N_REP * TABLES)
    base = UNIQ // N_REP
    spread = base // 4
    half = N_REP // 2

    def draw_pair(subkey):
        key_a, key_b, key_c, key_d = jax.random.split(subkey, 4)
        shifts = jax.random.randint(key_a, (half,), 0, spread + 1)
        widest = jax.random.randint(key_b, (), 0, half)
        shifts = jnp.where(jnp.arange(half, dtype=jnp.int32) == widest, spread, shifts)
        counts = jnp.stack([base + shifts, base - shifts], axis=1).reshape(N_REP).astype(jnp.int32)
        perm_keys = jax.random.split(key_c, N_REP)
        perms = jax.vmap(lambda one_key: jax.random.permutation(one_key, ROWS_DEV))(perm_keys).astype(jnp.int32)
        keeper_ids = jnp.arange(N_REP, dtype=jnp.int32)
        forced = jnp.where(keeper_ids == N_REP - 1, ROWS_DEV - 1, 0).astype(jnp.int32)
        pinned = perms[keeper_ids, forced]
        ranks = (perms - pinned[:, None]) % ROWS_DEV
        chosen = (ranks < counts[:, None]).reshape(ROWS)
        order = jax.random.permutation(key_d, ROWS).astype(jnp.int32)
        scores = jnp.where(chosen, order, ROWS + order)
        picked = jnp.argsort(scores, stable=True)[:UNIQ]
        return picked.astype(jnp.int32)
    return jax.vmap(draw_pair)(key_list).reshape(N_REP, TABLES, UNIQ).astype(jnp.int32)


def with_spikes(array, stream_key, source, target, blocks, factor):
    owner, partner = [(jnp.arange(array.shape[position]) // (array.shape[position] // blocks)).reshape([-1 if axis == position else 1 for axis in range(array.ndim)]) for position in (source, target)]
    chosen = jax.random.permutation(stream_key, blocks)[partner]
    strong = (owner == chosen) | (owner == (partner + blocks // 2) % blocks)
    return jnp.where(strong, factor * array, array)


def levels(key, extent, pieces, low, top_value):
    level, own = 1.0, jax.random.fold_in(key, 6)
    for axis_at, blocks in pieces:
        draws = jnp.exp(jax.random.uniform(jax.random.fold_in(own, axis_at), (blocks,), jnp.float32, low / len(pieces), top_value / len(pieces)))
        level = level * jnp.repeat(draws, extent[axis_at] // blocks).reshape([-1 if axis == axis_at else 1 for axis in range(len(extent))])
    return level


def gaussian(own_key, shape, scale, bound, cuts=(), kind=jnp.bfloat16):
    entries = jax.random.normal(own_key, shape, jnp.float32) * scale
    if len(cuts) > 0:
        entries = levels(own_key, shape, cuts, -0.22, 0.18) * entries
    return jnp.clip(entries, min=-bound, max=bound).astype(kind)


def gaussian_with(rng, shape, width, most, cuts, heavy, kind=jnp.bfloat16):
    result = width * jax.random.normal(rng, shape, jnp.float32)
    if cuts:
        result = result * levels(rng, shape, cuts, -0.22, 0.18)
    return jnp.clip(with_spikes(result, jax.random.fold_in(rng, 3), *heavy), -most, most).astype(kind)


def setup_inputs(seed: int = 0) -> dict:
    keys = jax.random.split(jax.random.key(seed), 9)
    dense_out = gaussian(keys[0], (SAMPLES, EMB), 1.0, 6.0, ((0, 256),))
    pooled = gaussian(keys[1], (SAMPLES, TABLES * EMB), 1.0, 6.0, ((0, 256),))
    cotangent = gaussian_with(keys[2], (SAMPLES, D0), 1.0, 24.0, ((0, 256),), (0, 1, 128, 5.5))
    proj_v = gaussian(keys[3], (D0, R), D0 ** -0.5, 0.125)
    proj_u = gaussian(keys[4], (R, D0), R ** -0.5, 0.3125)
    bias = gaussian(keys[5], (D0,), 0.5, 3.0, (), jnp.float32)
    lookup_slot = draw_lookup_slot(jax.random.fold_in(keys[8], 71), 0)
    uniq_rows = draw_uniq_rows(jax.random.fold_in(keys[8], 71), 0)
    return {"dense_out": dense_out, "pooled": pooled, "cotangent": cotangent, "proj_v": proj_v, "proj_u": proj_u, "bias": bias, "lookup_slot": lookup_slot, "uniq_rows": uniq_rows}


def reference(dense_out, pooled, cotangent, proj_v, proj_u, bias, lookup_slot, uniq_rows):
    grad_scale = float(SAMPLES) ** -0.5
    features = jnp.concatenate([dense_out, pooled], axis=1)
    latent = jnp.dot(features, proj_v, preferred_element_type=jnp.float32).astype(jnp.bfloat16)
    mixing = jnp.dot(latent, proj_u, preferred_element_type=jnp.float32) + bias
    grad_mix = (cotangent.astype(jnp.float32) * features.astype(jnp.float32)).astype(jnp.bfloat16)
    grad_latent = jnp.dot(grad_mix, proj_u.T, preferred_element_type=jnp.float32).astype(jnp.bfloat16)
    backward = jnp.dot(grad_latent, proj_v[EMB:].T, preferred_element_type=jnp.float32)
    pooled_grad = (cotangent[:, EMB:].astype(jnp.float32) * (mixing[:, EMB:] + 1.0) + backward).astype(jnp.bfloat16)
    grad_u = jnp.dot(latent.T, grad_mix, preferred_element_type=jnp.float32) * grad_scale
    grad_v = jnp.dot(features.T, grad_latent, preferred_element_type=jnp.float32) * grad_scale
    grad_bias = jnp.sum(grad_mix.astype(jnp.float32), axis=0) * grad_scale
    group_size = SAMPLES // N_REP
    group_of = (jnp.arange(SAMPLES, dtype=jnp.int32) // group_size).astype(jnp.int32)

    def per_table(table_idx):
        grads_t = lax.dynamic_slice_in_dim(pooled_grad, (table_idx * EMB).astype(jnp.int32), EMB, 1).astype(jnp.float32)
        slot_t = lax.dynamic_index_in_dim(lookup_slot, table_idx, 1, keepdims=False)
        uniq_t = lax.dynamic_index_in_dim(uniq_rows, table_idx, 1, keepdims=False)
        row_ids = uniq_t[group_of[:, None], slot_t]
        values = jnp.broadcast_to(grads_t[:, None, :], (SAMPLES, POOL, EMB)).reshape(SAMPLES * POOL, EMB)
        return jax.ops.segment_sum(values, row_ids.reshape(SAMPLES * POOL), num_segments=ROWS)

    row_grad = lax.map(per_table, jnp.arange(TABLES, dtype=jnp.int32))
    return grad_u, grad_v, grad_bias, row_grad
```

```python
import jax
import jax.numpy as jnp
import numpy as np
from jax import lax
from jax.experimental import pallas as pl
from jax.experimental.pallas import tpu as pltpu
from jax.sharding import Mesh, PartitionSpec as P

BF = jnp.bfloat16
F32 = jnp.float32
TABLE = ("zl", "y", "c")
REP = ("zh", "x")
EMB = 128
LAT = 384
N_TAB = 16
N_REP = 16
D0 = 2176
FEAT = 136
LATP = 24
KEEP = 512
CAP = 160
SLOTS = N_REP * CAP
PAYLOAD = CAP + 16
UNIQ = 2048
SAMP = 2048
SCALE = float(32768) ** -0.5

VMEM = pl.BlockSpec(memory_space=pltpu.VMEM)
SMEM = pl.BlockSpec(memory_space=pltpu.SMEM)
PARAMS = pltpu.CompilerParams(vmem_limit_bytes=56 * 1024 * 1024)


def nn(a, b):
    return lax.dot_general(a, b, (((1,), (0,)), ((), ())), preferred_element_type=F32)


def nt(a, b):
    return lax.dot_general(a, b, (((1,), (1,)), ((), ())), preferred_element_type=F32)


def tn(a, b):
    return lax.dot_general(a, b, (((0,), (0,)), ((), ())), preferred_element_type=F32)


def times(a, b):
    return (a.astype(F32) * b.astype(F32)).astype(BF)


def down(dense, pooled, cot, v_ref, u_ref):
    mix_dense = times(cot[:, :EMB], dense)
    mix_pooled = times(cot[:, EMB:], pooled)
    latent = (nn(dense, v_ref[:EMB, :]) + nn(pooled, v_ref[EMB:, :])).astype(BF)
    grad_latent = (nt(mix_dense, u_ref[:, :EMB]) + nt(mix_pooled, u_ref[:, EMB:])).astype(BF)
    return latent, grad_latent, mix_dense, mix_pooled


def front_kernel(dense_ref, pooled_ref, cot_ref, v_ref, u_ref, bias_ref, out_ref, lat_ref, gl_ref):
    latent, grad_latent, _, _ = down(dense_ref[...], pooled_ref[...], cot_ref[...], v_ref, u_ref)
    lat_ref[...] = latent
    gl_ref[...] = grad_latent
    for t in range(N_TAB):
        cols = slice(EMB + t * EMB, EMB + (t + 1) * EMB)
        mixing = nn(latent, u_ref[:, cols]) + bias_ref[:, cols]
        backward = nt(grad_latent, v_ref[cols, :])
        out_ref[t] = (cot_ref[:, cols].astype(F32) * (mixing + 1.0) + backward).astype(BF)


def weight_kernel(
    place_ref, dense_ref, pooled_ref, cot_ref, lat_ref, gl_ref, dense2_ref, pooled2_ref, cot2_ref,
    v_ref, u_ref, out0, out1, out2, out3, gu, gv, bias_row,
):
    lat2, gl2, md2, mp2 = down(dense2_ref[...], pooled2_ref[...], cot2_ref[...], v_ref, u_ref)
    lat = jnp.concatenate([lat_ref[...], lat2], axis=0)
    gl = jnp.concatenate([gl_ref[...], gl2], axis=0)
    for j in range(D0 // EMB):
        cols = slice(j * EMB, (j + 1) * EMB)
        prev = slice((j - 1) * EMB, j * EMB)
        feat1 = dense_ref[...] if j == 0 else pooled_ref[:, prev]
        feat2 = dense2_ref[...] if j == 0 else pooled2_ref[:, prev]
        mix1 = times(cot_ref[:, cols], feat1)
        mix2 = md2 if j == 0 else mp2[:, prev]
        mix = jnp.concatenate([mix1, mix2], axis=0)
        feat = jnp.concatenate([feat1, feat2], axis=0)
        gu[cols, :] = tn(mix, lat)
        gv[cols, :] = tn(feat, gl)
        bias_row[:, cols] = jnp.sum(mix.astype(F32), axis=0, keepdims=True)
    high = bias_row[...].astype(BF)
    low = (bias_row[...] - high.astype(F32)).astype(BF)
    tail = jnp.zeros((1, 6 * LAT - D0), BF)
    rows = []
    for part in (high, low):
        whole = jnp.concatenate([part, tail], axis=1)
        rows += [whole[:, k * LAT : (k + 1) * LAT].astype(F32) for k in range(6)]
    rows.append(jnp.zeros((4, LAT), F32))
    bias_block = jnp.concatenate(rows, axis=0).astype(BF)
    y, c = place_ref[0], place_ref[1]
    for s, out in enumerate((out0, out1, out2, out3)):
        dest_y = lax.rem(y + s, 4)
        for part, g in enumerate((gu, gv)):
            blocks = []
            for zl in range(2):
                start = pl.multiple_of((zl * 8 + dest_y * 2 + c) * FEAT, 8)
                blocks.append(g[pl.ds(start, FEAT), :])
            out[part * 272 : (part + 1) * 272, :] = jnp.concatenate(blocks, axis=0).astype(BF)
        out[544:560, :] = bias_block


def bias_again(block):
    total = block[0:6, :] + block[6:12, :]
    high = total.astype(BF).astype(F32)
    low = (total - high).astype(BF).astype(F32)
    return jnp.concatenate([high, low, jnp.zeros((4, LAT), F32)], axis=0)


def after_y_kernel(place_ref, m0, m1, m2, m3, keep_ref, send_ref, acc):
    acc[...] = (m0[...].astype(F32) + m1[...].astype(F32)) + (m2[...].astype(F32) + m3[...].astype(F32))
    zl = place_ref[2]
    bias = bias_again(acc[544:560, :])
    for out, half in ((keep_ref, zl), (send_ref, 1 - zl)):
        blocks = [
            acc[pl.ds(pl.multiple_of(part * 272 + half * FEAT, 8), FEAT), :] for part in range(2)
        ]
        out[0:272, :] = jnp.concatenate(blocks, axis=0).astype(out.dtype)
        out[272:288, :] = bias.astype(out.dtype)


def after_zl_kernel(place_ref, keep_ref, got_ref, out0, out1, out2, out3, flip):
    total = keep_ref[...] + got_ref[...].astype(F32)
    bias = bias_again(total[272:288, :]).astype(BF)
    stacked = jnp.concatenate(
        [total[0:128], total[136:264], total[128:136], total[264:272], jnp.zeros((112, LAT), F32)],
        axis=0,
    )
    flip[...] = stacked.T
    x = place_ref[3]
    for s, out in enumerate((out0, out1, out2, out3)):
        dest_x = lax.rem(x + s, 4)
        blocks = [
            flip[pl.ds(pl.multiple_of((zh * 4 + dest_x) * LATP, 8), LATP), :] for zh in range(4)
        ]
        out[0:96, :] = jnp.concatenate(blocks, axis=0).astype(BF)
        out[96:112, :] = bias


def after_x_kernel(place_ref, m0, m1, m2, m3, out0, out1, out2, out3, acc):
    acc[...] = (m0[...].astype(F32) + m1[...].astype(F32)) + (m2[...].astype(F32) + m3[...].astype(F32))
    bias = bias_again(acc[96:112, :]).astype(BF)
    zh = place_ref[4]
    for s, out in enumerate((out0, out1, out2, out3)):
        dest = lax.rem(zh + s, 4)
        block = acc[pl.ds(pl.multiple_of(dest * LATP, 8), LATP), :]
        out[0:32, :] = jnp.concatenate([block, jnp.zeros((8, LAT), F32)], axis=0).astype(BF)
        out[32:48, :] = bias


def last_kernel(m0, m1, m2, m3, u_ref, v_ref, bias_ref):
    total = (m0[...].astype(F32) + m1[...].astype(F32)) + (m2[...].astype(F32) + m3[...].astype(F32))
    total = total * SCALE
    u_ref[:, 0:128] = total[0:LATP, 0:128]
    u_ref[:, 128:136] = total[0:LATP, 256:264]
    v_ref[:, 0:128] = total[0:LATP, 128:256]
    v_ref[:, 128:136] = total[0:LATP, 264:272]
    bias = total[32:38, :] + total[38:44, :]
    for k in range(6):
        width = min(LAT, D0 - k * LAT)
        bias_ref[:, k * LAT : k * LAT + width] = bias[k : k + 1, 0:width]


def index_kernel(uniq_ref, slot_ref, hot_ref, pos_ref):
    uniq = uniq_ref[...]
    keeper = lax.shift_right_logical(uniq, 9)
    row = jnp.bitwise_and(uniq, KEEP - 1)
    upper = (
        lax.broadcasted_iota(jnp.int32, (128, 128), 0) <= lax.broadcasted_iota(jnp.int32, (128, 128), 1)
    ).astype(F32).astype(BF)
    which = lax.broadcasted_iota(jnp.int32, (N_REP, 128), 0)
    carry = jnp.zeros((N_REP, 1), F32)
    parts = []
    for b in range(UNIQ // 128):
        member = (which == keeper[:, b * 128 : (b + 1) * 128]).astype(F32)
        running = nn(member.astype(BF), upper) + carry
        carry = running[:, 127:128]
        place = member * (running - 1.0 + which.astype(F32) * float(CAP))
        parts.append(jnp.sum(place, axis=0, keepdims=True))
    dest = jnp.concatenate(parts, axis=1).astype(jnp.int32)
    zeros6 = jnp.zeros((6, UNIQ), F32)

    def digits(values, shift):
        low = jnp.bitwise_and(values, (1 << shift) - 1).astype(F32)
        high = lax.shift_right_logical(values, shift).astype(F32)
        return jnp.concatenate([high, low, zeros6], axis=0).astype(BF)

    dest_digits = digits(dest, 4)
    row_digits = digits(row, 4)
    found = []
    for p in range(2):
        acc = jnp.zeros((8, SAMP), F32)
        for b in range(UNIQ // 256):
            names = lax.broadcasted_iota(jnp.int32, (256, SAMP), 0) + b * 256
            hot = (names == slot_ref[p : p + 1, :]).astype(F32).astype(BF)
            acc = acc + nn(dest_digits[:, b * 256 : (b + 1) * 256], hot)
        found.append((acc[0:1, :] * 16.0 + acc[1:2, :]).astype(jnp.int32))
    for k in range(N_REP):
        places = lax.broadcasted_iota(jnp.int32, (CAP, SAMP), 0) + k * CAP
        first = (places == found[0]).astype(F32)
        hot_ref[k * CAP : (k + 1) * CAP, :] = (first + (places == found[1]).astype(F32)).astype(BF)
        listed = (places == dest).astype(F32).astype(BF)
        where = nt(row_digits, listed)
        wide = jnp.concatenate([where, jnp.zeros((8, 256 - CAP), F32)], axis=1)
        block = jnp.concatenate([wide[0:1, 0:128], wide[0:1, 128:256], wide[1:2, 0:128], wide[1:2, 128:256]], axis=0)
        pos_ref[k] = jnp.concatenate([block, jnp.zeros((12, 128), F32)], axis=0).astype(BF)


def rows_kernel(hot_ref, got_ref, pos_ref, out_ref):
    out_ref[0, 0:CAP, :] = nn(hot_ref[...], got_ref[...]).astype(BF)
    out_ref[0, CAP:PAYLOAD, :] = pos_ref[0]


def keep_kernel(got_ref, out_ref):
    names = lax.broadcasted_iota(jnp.int32, (KEEP, CAP), 0).astype(F32)
    acc = jnp.zeros((KEEP, EMB), F32)
    for g in range(N_REP):
        pos = got_ref[g, CAP:PAYLOAD, :].astype(F32)
        at = pos[0:2, :] * 16.0 + pos[2:4, :]
        at = jnp.concatenate([at[0:1, :], at[1:2, 0 : CAP - 128]], axis=1)
        hot = (names == at).astype(F32).astype(BF)
        acc = acc + nn(hot, got_ref[g, 0:CAP, :])
    out_ref[...] = acc


def call(kernel, outs, ins, scratch=(), place=True):
    specs = ([SMEM] if place else []) + [VMEM] * (len(ins) - (1 if place else 0))
    return pl.pallas_call(
        kernel,
        out_shape=tuple(jax.ShapeDtypeStruct(s, d) for s, d in outs),
        in_specs=specs,
        out_specs=tuple(VMEM for _ in outs),
        scratch_shapes=list(scratch),
        compiler_params=PARAMS,
    )(*ins)


def around(messages, axis):
    return [messages[0]] + [
        lax.ppermute(messages[s], axis, [(i, (i + s) % 4) for i in range(4)]) for s in (1, 2, 3)
    ]


def shards(dense, pooled, cot, proj_v, proj_u, bias, lookup_slot, uniq_rows):
    place = jnp.stack([lax.axis_index(a) for a in ("y", "c", "zl", "x", "zh")]).astype(jnp.int32)
    swap = [(0, 1), (1, 0)]
    other = [lax.ppermute(a, "c", swap) for a in (dense, pooled, cot)]
    outgoing, latent, grad_latent = call(
        front_kernel,
        [((N_TAB, 128, EMB), BF), ((128, LAT), BF), ((128, LAT), BF)],
        [dense, pooled, cot, proj_v, proj_u, bias.reshape(1, D0)],
        place=False,
    )
    received = lax.all_to_all(outgoing, TABLE, 0, 0, tiled=True).reshape(SAMP, EMB)
    slots = lookup_slot.reshape(SAMP, 2).T
    hot, pos = call(
        index_kernel,
        [((SLOTS, SAMP), BF), ((N_REP, 16, 128), BF)],
        [uniq_rows.reshape(1, UNIQ), slots],
        place=False,
    )
    message = ((560, LAT), BF)
    along_y = call(
        weight_kernel,
        [message] * 4,
        [place, dense, pooled, cot, latent, grad_latent, *other, proj_v, proj_u],
        [pltpu.VMEM((D0, LAT), F32), pltpu.VMEM((D0, LAT), F32), pltpu.VMEM((1, D0), F32)],
    )
    along_y = around(along_y, "y")
    payload = pl.pallas_call(
        rows_kernel,
        grid=(N_REP,),
        out_shape=jax.ShapeDtypeStruct((N_REP, PAYLOAD, EMB), BF),
        in_specs=[
            pl.BlockSpec((CAP, SAMP), lambda k: (k, 0)),
            pl.BlockSpec((SAMP, EMB), lambda k: (0, 0)),
            pl.BlockSpec((1, 16, 128), lambda k: (k, 0, 0)),
        ],
        out_specs=pl.BlockSpec((1, PAYLOAD, EMB), lambda k: (k, 0, 0)),
        compiler_params=PARAMS,
    )(hot, received, pos)
    gathered = lax.all_to_all(payload, REP, 0, 0, tiled=True)
    kept, sent = call(
        after_y_kernel,
        [((288, LAT), F32), ((288, LAT), BF)],
        [place, *along_y],
        [pltpu.VMEM((560, LAT), F32)],
    )
    got = lax.ppermute(sent, "zl", swap)
    along_x = call(
        after_zl_kernel, [((112, LAT), BF)] * 4, [place, kept, got], [pltpu.VMEM((LAT, LAT), F32)]
    )
    along_x = around(along_x, "x")
    along_z = call(
        after_x_kernel, [((48, LAT), BF)] * 4, [place, *along_x], [pltpu.VMEM((112, LAT), F32)]
    )
    along_z = around(along_z, "zh")
    part_u, part_v, whole_bias = call(
        last_kernel,
        [((LATP, FEAT), F32), ((LATP, FEAT), F32), ((1, D0), F32)],
        along_z,
        place=False,
    )
    (row_part,) = call(keep_kernel, [((KEEP, EMB), F32)], [gathered], place=False)
    return part_u, part_v.T, whole_bias.reshape(D0), row_part.reshape(1, KEEP, EMB)


def solution(mesh):
    fine = Mesh(np.asarray(mesh.devices).reshape(4, 4, 2, 4, 2), ("zh", "x", "zl", "y", "c"))
    every = P(REP + TABLE, None)
    placed = (every, every, every, P(), P(), P(), P(REP, TABLE, None), P(REP, TABLE, None))
    return jax.shard_map(
        shards,
        mesh=fine,
        in_specs=placed,
        out_specs=(P(REP, TABLE), P(TABLE, REP), P(), P(TABLE, REP, None)),
        check_vma=False,
    )
```

```python
import jax
import jax.numpy as jnp
import numpy as np
from jax import lax
from jax.experimental import pallas as pl
from jax.experimental.pallas import tpu as pltpu
from jax.sharding import Mesh, PartitionSpec as P

BF = jnp.bfloat16
F32 = jnp.float32
TABLE = ("zl", "y", "c")
REP = ("zh", "x")
EMB = 128
LAT = 384
N_TAB = 16
N_REP = 16
D0 = 2176
FEAT = 136
LATP = 24
KEEP = 512
CAP = 160
SLOTS = N_REP * CAP
PAYLOAD = CAP + 16
UNIQ = 2048
SAMP = 2048
SCALE = float(32768) ** -0.5

HBM = pl.BlockSpec(memory_space=pltpu.HBM)
ANY = pl.BlockSpec(memory_space=pl.ANY)
VMEM = pl.BlockSpec(memory_space=pltpu.VMEM)
SMEM = pl.BlockSpec(memory_space=pltpu.SMEM)


def params(mib):
    return pltpu.CompilerParams(vmem_limit_bytes=mib * 1024 * 1024)


def coords(place_ref):
    i = place_ref[0]
    return (
        lax.shift_right_logical(i, 6),
        jnp.bitwise_and(lax.shift_right_logical(i, 4), 3),
        jnp.bitwise_and(lax.shift_right_logical(i, 3), 1),
        jnp.bitwise_and(lax.shift_right_logical(i, 1), 3),
        jnp.bitwise_and(i, 1),
    )


def nn(a, b):
    return lax.dot_general(a, b, (((1,), (0,)), ((), ())), preferred_element_type=F32)


def nt(a, b):
    return lax.dot_general(a, b, (((1,), (1,)), ((), ())), preferred_element_type=F32)


def tn(a, b):
    return lax.dot_general(a, b, (((0,), (0,)), ((), ())), preferred_element_type=F32)


def times(a, b):
    return (a.astype(F32) * b.astype(F32)).astype(BF)


def front_kernel(
    dense_hbm, pooled_hbm, cot_hbm, v_hbm, u_hbm, bias_hbm, out_hbm, lat_ref, gl_ref,
    dense_ref, pooled_ref, cot_ref, v_ref, u_ref, bias_ref, out_ref, sems, out_sems,
):
    pairs = (
        (pooled_hbm, pooled_ref), (v_hbm, v_ref), (dense_hbm, dense_ref),
        (cot_hbm, cot_ref), (u_hbm, u_ref), (bias_hbm, bias_ref),
    )
    loads = [pltpu.make_async_copy(src, dst, sems.at[i]) for i, (src, dst) in enumerate(pairs)]
    for load in loads:
        load.start()
    for load in loads[:3]:
        load.wait()
    dense, pooled = dense_ref[...], pooled_ref[...]
    latent = (nn(dense, v_ref[:EMB, :]) + nn(pooled, v_ref[EMB:, :])).astype(BF)
    for load in loads[3:]:
        load.wait()
    mix_dense = times(cot_ref[:, :EMB], dense)
    mix_pooled = times(cot_ref[:, EMB:], pooled)
    grad_latent = (nt(mix_dense, u_ref[:, :EMB]) + nt(mix_pooled, u_ref[:, EMB:])).astype(BF)
    lat_ref[...] = latent
    gl_ref[...] = grad_latent
    stores = []
    for t in range(N_TAB):
        cols = slice(EMB + t * EMB, EMB + (t + 1) * EMB)
        mixing = nn(latent, u_ref[:, cols]) + bias_ref[t + 1 : t + 2, :]
        backward = nt(grad_latent, v_ref[cols, :])
        out_ref[t] = (cot_ref[:, cols].astype(F32) * (mixing + 1.0) + backward).astype(BF)
        if t % 4 == 3:
            some = slice(t - 3, t + 1)
            store = pltpu.make_async_copy(out_ref.at[some], out_hbm.at[some], out_sems.at[t // 4])
            store.start()
            stores.append(store)
    for store in stores:
        store.wait()


def order_kernel(*_):
    pass


def weight_kernel(
    place_ref, lat_ref, gl_ref, pooled2_hbm, v_hbm, dense2_hbm, cot2_hbm, u_hbm, pooled_hbm, cot_hbm, dense_hbm,
    u0, u1, u2, u3, v_keep, v_send,
    pooled2_ref, v_ref, dense2_ref, cot2_ref, u_ref, pooled_ref, cot_ref, dense_ref,
    gu, gv, bias_row, bu0, bu1, bu2, bu3, bk, bs, load_sems, sems,
):
    pairs = (
        (pooled2_hbm, pooled2_ref), (v_hbm, v_ref), (dense2_hbm, dense2_ref), (cot2_hbm, cot2_ref),
        (u_hbm, u_ref), (pooled_hbm, pooled_ref), (cot_hbm, cot_ref), (dense_hbm, dense_ref),
    )
    loads = [pltpu.make_async_copy(src, dst, load_sems.at[i]) for i, (src, dst) in enumerate(pairs)]
    for load in loads:
        load.start()
    for load in loads[:3]:
        load.wait()
    lat2 = (nn(dense2_ref[...], v_ref[:EMB, :]) + nn(pooled2_ref[...], v_ref[EMB:, :])).astype(BF)
    for load in loads[3:5]:
        load.wait()
    md2 = times(cot2_ref[:, :EMB], dense2_ref[...])
    mp2 = times(cot2_ref[:, EMB:], pooled2_ref[...])
    gl2 = (nt(md2, u_ref[:, :EMB]) + nt(mp2, u_ref[:, EMB:])).astype(BF)
    lat = jnp.concatenate([lat_ref[...], lat2], axis=0)
    gl = jnp.concatenate([gl_ref[...], gl2], axis=0)
    for load in loads[5:]:
        load.wait()
    for j in range(D0 // EMB):
        cols = slice(j * EMB, (j + 1) * EMB)
        prev = slice((j - 1) * EMB, j * EMB)
        feat1 = dense_ref[...] if j == 0 else pooled_ref[:, prev]
        feat2 = dense2_ref[...] if j == 0 else pooled2_ref[:, prev]
        mix1 = times(cot_ref[:, cols], feat1)
        mix2 = md2 if j == 0 else mp2[:, prev]
        mix = jnp.concatenate([mix1, mix2], axis=0)
        feat = jnp.concatenate([feat1, feat2], axis=0)
        gu[cols, :] = tn(mix, lat)
        gv[cols, :] = tn(feat, gl)
        bias_row[:, cols] = jnp.sum(mix.astype(F32), axis=0, keepdims=True)
    high = bias_row[...].astype(BF)
    low = (bias_row[...] - high.astype(F32)).astype(BF)
    tail = jnp.zeros((1, 6 * LAT - D0), BF)
    rows = []
    for part in (high, low):
        whole = jnp.concatenate([part, tail], axis=1)
        rows += [whole[:, k * LAT : (k + 1) * LAT].astype(F32) for k in range(6)]
    rows.append(jnp.zeros((4, LAT), F32))
    bias_block = jnp.concatenate(rows, axis=0).astype(BF)
    _, _, zl, y, c = coords(place_ref)
    copies = []

    def block(g, zl, y):
        start = pl.multiple_of((zl * 8 + y * 2 + c) * FEAT, 8)
        return g[pl.ds(start, FEAT), :]

    def leave(buffer, out):
        copy = pltpu.make_async_copy(buffer, out, sems.at[len(copies)])
        copy.start()
        copies.append(copy)

    for s, (buffer, out) in enumerate(((bu0, u0), (bu1, u1), (bu2, u2), (bu3, u3))):
        dest_y = lax.rem(y + s, 4)
        buffer[0:272, :] = jnp.concatenate([block(gu, 0, dest_y), block(gu, 1, dest_y)], axis=0).astype(BF)
        buffer[272:288, :] = bias_block
        leave(buffer, out)
    for half, buffer, out in ((zl, bk, v_keep), (1 - zl, bs, v_send)):
        for i in range(2):
            pair = jnp.concatenate([block(gv, half, 2 * i), block(gv, half, 2 * i + 1)], axis=0)
            buffer[i * 272 : (i + 1) * 272, :] = pair.astype(BF)
        leave(buffer, out)
    for copy in copies:
        copy.wait()


def bias_again(block):
    total = block[0:6, :] + block[6:12, :]
    high = total.astype(BF).astype(F32)
    low = (total - high).astype(BF).astype(F32)
    return jnp.concatenate([high, low, jnp.zeros((4, LAT), F32)], axis=0)


def first_sum_kernel(
    place_ref, m0, m1, m2, m3, v_own, v_got, _, u_keep, u_send, v0, v1, v2, v3,
    acc_u, acc_v, bs, b1, b2, b3, sems,
):
    acc_u[...] = (m0[...].astype(F32) + m1[...].astype(F32)) + (m2[...].astype(F32) + m3[...].astype(F32))
    acc_v[...] = v_own[...].astype(F32) + v_got[...].astype(F32)
    _, _, zl, y, _ = coords(place_ref)
    bias = bias_again(acc_u[272:288, :])
    gap = jnp.zeros((8, LAT), F32)
    copies = []

    def leave(buffer, out):
        copy = pltpu.make_async_copy(buffer, out, sems.at[len(copies)])
        copy.start()
        copies.append(copy)

    bs[...] = jnp.concatenate(
        [acc_u[pl.ds(pl.multiple_of((1 - zl) * FEAT, 8), FEAT), :], gap, bias], axis=0
    ).astype(BF)
    leave(bs, u_send)
    for s, buffer, out in ((1, b1, v1), (2, b2, v2), (3, b3, v3)):
        start = pl.multiple_of(lax.rem(y + s, 4) * FEAT, 8)
        buffer[...] = jnp.concatenate([acc_v[pl.ds(start, FEAT), :], gap], axis=0).astype(BF)
        leave(buffer, out)
    u_keep[...] = jnp.concatenate(
        [acc_u[pl.ds(pl.multiple_of(zl * FEAT, 8), FEAT), :], gap, bias], axis=0
    )
    v0[...] = jnp.concatenate([acc_v[pl.ds(pl.multiple_of(y * FEAT, 8), FEAT), :], gap], axis=0)
    for copy in copies:
        copy.wait()


def pick(ref, starts, rows):
    return [ref[pl.ds(pl.multiple_of(start, 8), rows), :] for start in starts]


def split(keep_ref, send_ref, buffer, sem, kept, sent):
    buffer[...] = jnp.concatenate(sent, axis=0).astype(BF)
    copy = pltpu.make_async_copy(buffer, send_ref, sem.at[0])
    copy.start()
    keep_ref[...] = jnp.concatenate(kept, axis=0)
    copy.wait()


def second_sum_kernel(
    place_ref, u_keep, u_got, v0, v1, v2, v3, keep_ref, send_ref, flip, buffer, sem
):
    u = u_keep[...] + u_got[...].astype(F32)
    v = (v0[...] + v1[...].astype(F32)) + (v2[...].astype(F32) + v3[...].astype(F32))
    bias = bias_again(u[144:160, :])
    stacked = jnp.concatenate(
        [u[0:128], v[0:128], u[128:136], v[128:136], jnp.zeros((112, LAT), F32)], axis=0
    )
    flip[...] = stacked.T
    _, x, _, _, _ = coords(place_ref)

    def rows_of(dest_x):
        return pick(flip, [(zh * 4 + dest_x) * LATP for zh in range(4)], LATP)

    kept = rows_of(x) + rows_of(3 - x) + [bias]
    sent = rows_of(jnp.bitwise_xor(x, 1)) + rows_of(jnp.bitwise_xor(x, 2)) + [bias]
    split(keep_ref, send_ref, buffer, sem, kept, sent)


def third_sum_kernel(_, keep, got, keep_ref, send_ref, acc, buffer, sem):
    acc[...] = keep[...] + got[...].astype(F32)
    bias = bias_again(acc[192:208, :])
    split(keep_ref, send_ref, buffer, sem, [acc[0:96, :], bias], [acc[96:192, :], bias])


def fourth_sum_kernel(place_ref, keep, got, keep_ref, send_ref, acc, buffer, sem):
    acc[...] = keep[...] + got[...].astype(F32)
    bias = bias_again(acc[96:112, :])
    zh, _, _, _, _ = coords(place_ref)
    kept = pick(acc, [zh * LATP, (3 - zh) * LATP], LATP)
    sent = pick(acc, [jnp.bitwise_xor(zh, 1) * LATP, jnp.bitwise_xor(zh, 2) * LATP], LATP)
    split(keep_ref, send_ref, buffer, sem, kept + [bias], sent + [bias])


def fifth_sum_kernel(_, keep, got, keep_ref, send_ref, acc, buffer, sem):
    acc[...] = keep[...] + got[...].astype(F32)
    bias = bias_again(acc[48:64, :])
    gap = jnp.zeros((8, LAT), F32)
    split(keep_ref, send_ref, buffer, sem, [acc[0:24, :], gap, bias], [acc[24:48, :], gap, bias])


def last_kernel(keep, got, u_ref, v_ref, bias_ref):
    total = keep[...] + got[...].astype(F32)
    total = total * SCALE
    u_ref[:, 0:128] = total[0:LATP, 0:128]
    u_ref[:, 128:136] = total[0:LATP, 256:264]
    v_ref[:, 0:128] = total[0:LATP, 128:256]
    v_ref[:, 128:136] = total[0:LATP, 264:272]
    bias = total[32:38, :] + total[38:44, :]
    for j in range(D0 // 128):
        k, at = j // 3, (j % 3) * 128
        bias_ref[j : j + 1, :] = bias[k : k + 1, at : at + 128]


def index_kernel(uniq_ref, slot_ref, found_ref, pos_ref):
    uniq = uniq_ref[...]
    keeper = lax.shift_right_logical(uniq, 9)
    row = jnp.bitwise_and(uniq, KEEP - 1)
    upper = (
        lax.broadcasted_iota(jnp.int32, (128, 128), 0) <= lax.broadcasted_iota(jnp.int32, (128, 128), 1)
    ).astype(F32).astype(BF)
    which = lax.broadcasted_iota(jnp.int32, (N_REP, 128), 0)
    carry = jnp.zeros((N_REP, 1), F32)
    members, ranks, keepers = [], [], []
    for b in range(UNIQ // 128):
        own = keeper[:, b * 128 : (b + 1) * 128]
        member = (which == own).astype(F32)
        running = nn(member.astype(BF), upper) + carry
        carry = running[:, 127:128]
        members.append(member)
        keepers.append(own.astype(F32))
        ranks.append(jnp.sum(member * (running - 1.0), axis=0, keepdims=True))
    member = jnp.concatenate(members, axis=1)
    rank = jnp.concatenate(ranks, axis=1)
    row_high = lax.shift_right_logical(row, 4).astype(F32)
    row_low = jnp.bitwise_and(row, 15).astype(F32)
    digits = jnp.concatenate([member * row_high, member * row_low], axis=0).astype(BF)
    ranked = lax.broadcasted_iota(jnp.int32, (CAP, UNIQ), 0).astype(F32) == rank
    where = nt(digits, ranked.astype(F32).astype(BF))
    wide = jnp.concatenate([where, jnp.zeros((2 * N_REP, 256 - CAP), F32)], axis=1)
    for k in range(N_REP):
        high, low = wide[k : k + 1, :], wide[N_REP + k : N_REP + k + 1, :]
        block = [high[:, 0:128], high[:, 128:256], low[:, 0:128], low[:, 128:256]]
        pos_ref[k] = jnp.concatenate(block + [jnp.zeros((12, 128), F32)], axis=0).astype(BF)
    table = jnp.concatenate(ranks + keepers, axis=0).astype(BF)
    found = []
    for p in range(2):
        slot = slot_ref[p : p + 1, :]
        low = jnp.bitwise_and(slot, 127)
        high = lax.shift_right_logical(slot, 7)
        hot_low = (lax.broadcasted_iota(jnp.int32, (128, SAMP), 0) == low).astype(F32).astype(BF)
        picked = nn(table, hot_low)
        hot_high = (lax.broadcasted_iota(jnp.int32, (16, SAMP), 0) == high).astype(F32)
        found.append(
            (
                jnp.sum(hot_high * picked[0:16, :], axis=0, keepdims=True),
                jnp.sum(hot_high * picked[16:32, :], axis=0, keepdims=True),
            )
        )
    rows = [row for pair in found for row in pair]
    found_ref[...] = jnp.concatenate(rows + [jnp.zeros((4, SAMP), F32)], axis=0)


def rows_kernel(found_ref, got_ref, pos_ref, out_hbm, hot, out_ref, sems):
    places = lax.broadcasted_iota(jnp.int32, (CAP, SAMP), 0).astype(F32).astype(BF)
    one, zero = jnp.ones((CAP, SAMP), BF), jnp.zeros((CAP, SAMP), BF)
    stores = []
    for j in range(4):
        for i in range(4):
            k = j * 4 + i
            hits = []
            for p in range(2):
                at, kept = found_ref[2 * p : 2 * p + 1, :], found_ref[2 * p + 1 : 2 * p + 2, :]
                own = jnp.where(kept == float(k), at, -1.0).astype(BF)
                hits.append(jnp.where(places == own, one, zero))
            hot[j % 2, i * CAP : (i + 1) * CAP, :] = hits[0] + hits[1]
        sums = nn(hot[j % 2], got_ref[...]).astype(BF)
        for i in range(4):
            k = j * 4 + i
            out_ref[k, 0:CAP, :] = sums[i * CAP : (i + 1) * CAP, :]
            out_ref[k, CAP:PAYLOAD, :] = pos_ref[k]
        some = slice(j * 4, j * 4 + 4)
        store = pltpu.make_async_copy(out_ref.at[some], out_hbm.at[some], sems.at[j])
        store.start()
        stores.append(store)
    for store in stores:
        store.wait()


def keep_kernel(got_ref, out_ref):
    names = lax.broadcasted_iota(jnp.int32, (KEEP, CAP), 0).astype(F32)
    acc = jnp.zeros((KEEP, EMB), F32)
    for g in range(N_REP):
        pos = got_ref[g, CAP:PAYLOAD, :].astype(F32)
        at = pos[0:2, :] * 16.0 + pos[2:4, :]
        at = jnp.concatenate([at[0:1, :], at[1:2, 0 : CAP - 128]], axis=1)
        hot = (names == at).astype(F32).astype(BF)
        acc = acc + nn(hot, got_ref[g, 0:CAP, :])
    out_ref[...] = acc


def call(kernel, outs, ins, scratch=(), mib=24, spare=None, us=2):
    return pl.pallas_call(
        kernel,
        out_shape=tuple(jax.ShapeDtypeStruct(s, d) for _, s, d in outs),
        in_specs=[spec for spec, _ in ins],
        out_specs=tuple(spec for spec, _, _ in outs),
        scratch_shapes=list(scratch),
        input_output_aliases={} if spare is None else {spare[0]: spare[1]},
        compiler_params=params(mib),
        cost_estimate=pl.CostEstimate(flops=us * 10**9, bytes_accessed=us * 10**6, transcendentals=0),
    )(*[a for _, a in ins])


def near(*arrays):
    return [(VMEM, a) for a in arrays]


def shifted(messages, axis):
    return [
        lax.ppermute(m, axis, [(i, (i + s) % 4) for i in range(4)]) for s, m in enumerate(messages, 1)
    ]


def shards(dense, pooled, cot, proj_v, proj_u, bias, lookup_slot, uniq_rows):
    place = (SMEM, lax.axis_index(REP + TABLE).astype(jnp.int32).reshape(1))
    swap = [(0, 1), (1, 0)]
    other = [lax.ppermute(a, "c", swap) for a in (dense, pooled, cot)]
    dma = pltpu.SemaphoreType.DMA
    weights = [(HBM, a) for a in (dense, pooled, cot, proj_v, proj_u)]
    bias_rows = (D0 // 128, 128)
    outgoing, latent, grad_latent = call(
        front_kernel,
        [(HBM, (N_TAB, 128, EMB), BF), (VMEM, (128, LAT), BF), (VMEM, (128, LAT), BF)],
        weights + [(HBM, bias.reshape(bias_rows))],
        [pltpu.VMEM(a.shape, BF) for _, a in weights]
        + [pltpu.VMEM(bias_rows, F32), pltpu.VMEM((N_TAB, 128, EMB), BF), dma((6,)), dma((4,))],
        mib=56,
        us=5,
    )
    (outgoing,) = call(
        order_kernel,
        [(HBM, outgoing.shape, BF)],
        [(HBM, outgoing)] + [(ANY, a) for a in other],
        spare=(0, 0),
    )
    received = lax.all_to_all(outgoing, TABLE, 0, 0, tiled=True).reshape(SAMP, EMB)
    u_shape, v_shape = (288, LAT), (544, LAT)
    dense2, pooled2, cot2 = other
    loaded = (pooled2, proj_v, dense2, cot2, proj_u, pooled, cot, dense)
    u0, u1, u2, u3, v_keep, v_send = call(
        weight_kernel,
        [(HBM, u_shape, BF)] * 4 + [(HBM, v_shape, BF)] * 2,
        [place] + near(latent, grad_latent) + [(HBM, a) for a in loaded],
        [pltpu.VMEM(a.shape, BF) for a in loaded]
        + [pltpu.VMEM((D0, LAT), F32), pltpu.VMEM((D0, LAT), F32), pltpu.VMEM((1, D0), F32)]
        + [pltpu.VMEM(u_shape, BF)] * 4
        + [pltpu.VMEM(v_shape, BF)] * 2
        + [dma((8,)), dma((6,))],
        mib=56,
        us=5,
    )
    u_got = shifted([u1, u2, u3], "y")
    v_got = lax.ppermute(v_send, "zl", swap)
    found, pos = call(
        index_kernel,
        [(VMEM, (8, SAMP), F32), (VMEM, (N_REP, 16, 128), BF)],
        near(uniq_rows.reshape(1, UNIQ), lookup_slot.reshape(SAMP, 2).T),
    )
    (payload,) = call(
        rows_kernel,
        [(HBM, (N_REP, PAYLOAD, EMB), BF)],
        near(found, received, pos),
        [pltpu.VMEM((2, 4 * CAP, SAMP), BF), pltpu.VMEM((N_REP, PAYLOAD, EMB), BF), dma((4,))],
        us=7,
    )
    u_shape, v_shape = (160, LAT), (144, LAT)
    u_keep, u_send, v0, v1, v2, v3 = call(
        first_sum_kernel,
        [(VMEM, u_shape, F32), (HBM, u_shape, BF), (VMEM, v_shape, F32)] + [(HBM, v_shape, BF)] * 3,
        [place] + near(u0, *u_got, v_keep, v_got) + [(ANY, payload)],
        [pltpu.VMEM((288, LAT), F32), pltpu.VMEM((544, LAT), F32), pltpu.VMEM(u_shape, BF)]
        + [pltpu.VMEM(v_shape, BF)] * 3
        + [dma((4,))],
    )
    (payload,) = call(
        order_kernel, [(HBM, payload.shape, BF)], [(HBM, payload), (ANY, u_keep)], spare=(0, 0)
    )
    gathered = lax.all_to_all(payload, REP, 0, 0, tiled=True)
    u_got = lax.ppermute(u_send, "zl", swap)
    v_got = shifted([v1, v2, v3], "y")
    flat = [(0, 1), (1, 0), (2, 3), (3, 2)]
    cross = [(0, 3), (3, 0), (1, 2), (2, 1)]

    def halve(kernel, ins, in_rows, rows, axis, pairs, us=2):
        kept, sent = call(
            kernel,
            [(VMEM, (rows, LAT), F32), (HBM, (rows, LAT), BF)],
            [place] + near(*ins),
            [pltpu.VMEM((in_rows, LAT), F32), pltpu.VMEM((rows, LAT), BF), dma((1,))],
            us=us,
        )
        return kept, lax.ppermute(sent, axis, pairs)

    both = halve(second_sum_kernel, (u_keep, u_got, v0, *v_got), LAT, 208, "x", flat, us=100)
    both = halve(third_sum_kernel, both, 208, 112, "x", cross)
    both = halve(fourth_sum_kernel, both, 112, 64, "zh", flat)
    both = halve(fifth_sum_kernel, both, 64, 48, "zh", cross)
    part_u, part_v, whole_bias = call(
        last_kernel,
        [(VMEM, (LATP, FEAT), F32), (VMEM, (LATP, FEAT), F32), (VMEM, (D0 // 128, 128), F32)],
        near(*both),
    )
    (row_part,) = call(keep_kernel, [(VMEM, (KEEP, EMB), F32)], near(gathered))
    return part_u, part_v.T, whole_bias.reshape(D0), row_part.reshape(1, KEEP, EMB)


def solution(mesh):
    fine = Mesh(np.asarray(mesh.devices).reshape(4, 4, 2, 4, 2), ("zh", "x", "zl", "y", "c"))
    every = P(REP + TABLE, None)
    placed = (every, every, every, P(), P(), P(), P(REP, TABLE, None), P(REP, TABLE, None))
    return jax.shard_map(
        shards,
        mesh=fine,
        in_specs=placed,
        out_specs=(P(REP, TABLE), P(TABLE, REP), P(), P(TABLE, REP, None)),
        check_vma=False,
    )
```

```python
import jax
import jax.numpy as jnp
import numpy as np
from jax import lax
from jax.experimental import pallas as pl
from jax.experimental.pallas import tpu as pltpu
from jax.sharding import Mesh, PartitionSpec as P

BF = jnp.bfloat16
F32 = jnp.float32
TABLE = ("zl", "y", "c")
REP = ("zh", "x")
EMB = 128
LAT = 384
N_TAB = 16
N_REP = 16
D0 = 2176
FEAT = 136
LATP = 24
KEEP = 512
CAP = 160
SLOTS = N_REP * CAP
PAYLOAD = CAP + 16
UNIQ = 2048
SAMP = 2048
SCALE = float(32768) ** -0.5

HBM = pl.BlockSpec(memory_space=pltpu.HBM)
ANY = pl.BlockSpec(memory_space=pl.ANY)
VMEM = pl.BlockSpec(memory_space=pltpu.VMEM)
SMEM = pl.BlockSpec(memory_space=pltpu.SMEM)


def params(mib):
    return pltpu.CompilerParams(vmem_limit_bytes=mib * 1024 * 1024)


def coords(place_ref):
    i = place_ref[0]
    return (
        lax.shift_right_logical(i, 6),
        jnp.bitwise_and(lax.shift_right_logical(i, 4), 3),
        jnp.bitwise_and(lax.shift_right_logical(i, 3), 1),
        jnp.bitwise_and(lax.shift_right_logical(i, 1), 3),
        jnp.bitwise_and(i, 1),
    )


def nn(a, b):
    return lax.dot_general(a, b, (((1,), (0,)), ((), ())), preferred_element_type=F32)


def nt(a, b):
    return lax.dot_general(a, b, (((1,), (1,)), ((), ())), preferred_element_type=F32)


def tn(a, b):
    return lax.dot_general(a, b, (((0,), (0,)), ((), ())), preferred_element_type=F32)


def times(a, b):
    return (a.astype(F32) * b.astype(F32)).astype(BF)


def pooled_kernel(
    lat_ref, gl_ref, cot_hbm, v_hbm, u_hbm, bias_hbm, out_hbm,
    cot_ref, v_ref, u_ref, bias_ref, out_ref, sems, v_sems, u_sems, out_sems,
):
    loads = [
        pltpu.make_async_copy(cot_hbm, cot_ref, sems.at[0]),
        pltpu.make_async_copy(bias_hbm, bias_ref, sems.at[1]),
    ]
    parts = []
    for j in range(4):
        cols = slice(EMB + j * 512, EMB + (j + 1) * 512)
        parts.append(
            (
                pltpu.make_async_copy(u_hbm.at[:, cols], u_ref.at[:, cols], u_sems.at[j]),
                pltpu.make_async_copy(v_hbm.at[cols, :], v_ref.at[cols, :], v_sems.at[j]),
            )
        )
    for copy in (*parts[0], *loads, *parts[1], *parts[2], *parts[3]):
        copy.start()
    latent, grad_latent = lat_ref[...], gl_ref[...]
    for load in loads:
        load.wait()
    stores = []
    for t in range(N_TAB):
        if t % 4 == 0:
            for part in parts[t // 4]:
                part.wait()
        cols = slice(EMB + t * EMB, EMB + (t + 1) * EMB)
        mixing = nn(latent, u_ref[:, cols]) + bias_ref[t + 1 : t + 2, :]
        backward = nt(grad_latent, v_ref[cols, :])
        out_ref[t] = (cot_ref[:, cols].astype(F32) * (mixing + 1.0) + backward).astype(BF)
        if t % 4 == 3:
            some = slice(t - 3, t + 1)
            store = pltpu.make_async_copy(out_ref.at[some], out_hbm.at[some], out_sems.at[t // 4])
            store.start()
            stores.append(store)
    for store in stores:
        store.wait()


def weight_kernel(
    place_ref, pooled_hbm, pooled2_hbm, dense_hbm, dense2_hbm, v_hbm, cot_hbm, cot2_hbm, u_hbm, _,
    u0, u1, u2, u3, v_keep, v_send, lat_ref, gl_ref,
    pooled_ref, dense_ref, cot_ref, mix_ref, v_ref, u_ref,
    gu, gv, bias_row, bu0, bu1, bu2, bu3, bk, bs, load_sems, sems,
):
    own, other = slice(0, 128), slice(128, 256)
    pairs = (
        (pooled_hbm, pooled_ref.at[own, :]), (pooled2_hbm, pooled_ref.at[other, :]),
        (dense_hbm, dense_ref.at[own, :]), (dense2_hbm, dense_ref.at[other, :]),
        (v_hbm, v_ref), (cot_hbm, cot_ref.at[own, :]), (cot2_hbm, cot_ref.at[other, :]), (u_hbm, u_ref),
    )
    loads = [pltpu.make_async_copy(src, dst, load_sems.at[i]) for i, (src, dst) in enumerate(pairs)]
    for load in loads:
        load.start()
    for load in loads[:5]:
        load.wait()
    lat = (nn(dense_ref[...], v_ref[:EMB, :]) + nn(pooled_ref[...], v_ref[EMB:, :])).astype(BF)
    for load in loads[5:7]:
        load.wait()
    mix_ref[:, :EMB] = times(cot_ref[:, :EMB], dense_ref[...])
    mix_ref[:, EMB:] = times(cot_ref[:, EMB:], pooled_ref[...])
    loads[7].wait()
    gl = nt(mix_ref[...], u_ref[...]).astype(BF)
    lat_ref[...] = lat[0:128, :]
    gl_ref[...] = gl[0:128, :]
    for j in range(D0 // EMB):
        cols = slice(j * EMB, (j + 1) * EMB)
        mix = mix_ref[:, cols]
        feat = dense_ref[...] if j == 0 else pooled_ref[:, (j - 1) * EMB : j * EMB]
        gu[cols, :] = tn(mix, lat)
        gv[cols, :] = tn(feat, gl)
        bias_row[:, cols] = jnp.sum(mix.astype(F32), axis=0, keepdims=True)
    high = bias_row[...].astype(BF)
    low = (bias_row[...] - high.astype(F32)).astype(BF)
    tail = jnp.zeros((1, 6 * LAT - D0), BF)
    rows = []
    for part in (high, low):
        whole = jnp.concatenate([part, tail], axis=1)
        rows += [whole[:, k * LAT : (k + 1) * LAT].astype(F32) for k in range(6)]
    rows.append(jnp.zeros((4, LAT), F32))
    bias_block = jnp.concatenate(rows, axis=0).astype(BF)
    _, _, zl, y, c = coords(place_ref)
    copies = []

    def block(g, zl, y):
        start = pl.multiple_of((zl * 8 + y * 2 + c) * FEAT, 8)
        return g[pl.ds(start, FEAT), :]

    def leave(buffer, out):
        copy = pltpu.make_async_copy(buffer, out, sems.at[len(copies)])
        copy.start()
        copies.append(copy)

    for s, (buffer, out) in enumerate(((bu0, u0), (bu1, u1), (bu2, u2), (bu3, u3))):
        dest_y = lax.rem(y + s, 4)
        buffer[0:272, :] = jnp.concatenate([block(gu, 0, dest_y), block(gu, 1, dest_y)], axis=0).astype(BF)
        buffer[272:288, :] = bias_block
        leave(buffer, out)
    for half, buffer, out in ((zl, bk, v_keep), (1 - zl, bs, v_send)):
        for i in range(2):
            pair = jnp.concatenate([block(gv, half, 2 * i), block(gv, half, 2 * i + 1)], axis=0)
            buffer[i * 272 : (i + 1) * 272, :] = pair.astype(BF)
        leave(buffer, out)
    for copy in copies:
        copy.wait()


def bias_again(block):
    total = block[0:6, :] + block[6:12, :]
    high = total.astype(BF).astype(F32)
    low = (total - high).astype(BF).astype(F32)
    return jnp.concatenate([high, low, jnp.zeros((4, LAT), F32)], axis=0)


def first_sum_kernel(
    place_ref, m0, m1, m2, m3, v_own, v_got, u_keep, u_send, v0, v1, v2, v3,
    acc_u, acc_v, bs, b1, b2, b3, sems,
):
    acc_u[...] = (m0[...].astype(F32) + m1[...].astype(F32)) + (m2[...].astype(F32) + m3[...].astype(F32))
    acc_v[...] = v_own[...].astype(F32) + v_got[...].astype(F32)
    _, _, zl, y, _ = coords(place_ref)
    bias = bias_again(acc_u[272:288, :])
    gap = jnp.zeros((8, LAT), F32)
    copies = []

    def leave(buffer, out):
        copy = pltpu.make_async_copy(buffer, out, sems.at[len(copies)])
        copy.start()
        copies.append(copy)

    bs[...] = jnp.concatenate(
        [acc_u[pl.ds(pl.multiple_of((1 - zl) * FEAT, 8), FEAT), :], gap, bias], axis=0
    ).astype(BF)
    leave(bs, u_send)
    for s, buffer, out in ((1, b1, v1), (2, b2, v2), (3, b3, v3)):
        start = pl.multiple_of(lax.rem(y + s, 4) * FEAT, 8)
        buffer[...] = jnp.concatenate([acc_v[pl.ds(start, FEAT), :], gap], axis=0).astype(BF)
        leave(buffer, out)
    u_keep[...] = jnp.concatenate(
        [acc_u[pl.ds(pl.multiple_of(zl * FEAT, 8), FEAT), :], gap, bias], axis=0
    )
    v0[...] = jnp.concatenate([acc_v[pl.ds(pl.multiple_of(y * FEAT, 8), FEAT), :], gap], axis=0)
    for copy in copies:
        copy.wait()


def pick(ref, starts, rows):
    return [ref[pl.ds(pl.multiple_of(start, 8), rows), :] for start in starts]


def split(keep_ref, send_ref, buffer, sem, kept, sent):
    buffer[...] = jnp.concatenate(sent, axis=0).astype(BF)
    copy = pltpu.make_async_copy(buffer, send_ref, sem.at[0])
    copy.start()
    keep_ref[...] = jnp.concatenate(kept, axis=0)
    copy.wait()


def second_sum_kernel(
    place_ref, u_keep, u_got, v0, v1, v2, v3, _, keep_ref, send_ref, flip, buffer, sem
):
    u = u_keep[...] + u_got[...].astype(F32)
    v = (v0[...] + v1[...].astype(F32)) + (v2[...].astype(F32) + v3[...].astype(F32))
    bias = bias_again(u[144:160, :])
    stacked = jnp.concatenate(
        [u[0:128], v[0:128], u[128:136], v[128:136], jnp.zeros((112, LAT), F32)], axis=0
    )
    flip[...] = stacked.T
    zh, x, _, _, _ = coords(place_ref)

    def rows_of(dest):
        order = (x, 3 - x, jnp.bitwise_xor(x, 1), jnp.bitwise_xor(x, 2))
        return pick(flip, [(dest * 4 + dest_x) * LATP for dest_x in order], LATP)

    kept = rows_of(zh) + rows_of(3 - zh) + [bias]
    sent = rows_of(jnp.bitwise_xor(zh, 1)) + rows_of(jnp.bitwise_xor(zh, 2)) + [bias]
    split(keep_ref, send_ref, buffer, sem, kept, sent)


def third_sum_kernel(_, keep, got, keep_ref, send_ref, acc, buffer, sem):
    acc[...] = keep[...] + got[...].astype(F32)
    bias = bias_again(acc[192:208, :])
    kept = [acc[0:48, :], acc[96:144, :], bias]
    split(keep_ref, send_ref, buffer, sem, kept, [acc[48:96, :], acc[144:192, :], bias])


def fourth_sum_kernel(_, keep, got, keep_ref, send_ref, acc, buffer, sem):
    acc[...] = keep[...] + got[...].astype(F32)
    bias = bias_again(acc[96:112, :])
    kept = [acc[0:24, :], acc[48:72, :], bias]
    split(keep_ref, send_ref, buffer, sem, kept, [acc[24:48, :], acc[72:96, :], bias])


def fifth_sum_kernel(_, keep, got, keep_ref, send_ref, acc, buffer, sem):
    acc[...] = keep[...] + got[...].astype(F32)
    bias = bias_again(acc[48:64, :])
    gap = jnp.zeros((8, LAT), F32)
    split(keep_ref, send_ref, buffer, sem, [acc[0:24, :], gap, bias], [acc[24:48, :], gap, bias])


def last_kernel(keep, got, u_ref, v_ref, bias_ref):
    total = keep[...] + got[...].astype(F32)
    total = total * SCALE
    u_ref[:, 0:128] = total[0:LATP, 0:128]
    u_ref[:, 128:136] = total[0:LATP, 256:264]
    v_ref[:, 0:128] = total[0:LATP, 128:256]
    v_ref[:, 128:136] = total[0:LATP, 264:272]
    bias = total[32:38, :] + total[38:44, :]
    for j in range(D0 // 128):
        k, at = j // 3, (j % 3) * 128
        bias_ref[j : j + 1, :] = bias[k : k + 1, at : at + 128]


def index_kernel(uniq_ref, slot_ref, found_ref, pos_ref):
    uniq = uniq_ref[...]
    keeper = lax.shift_right_logical(uniq, 9)
    row = jnp.bitwise_and(uniq, KEEP - 1)
    upper = (
        lax.broadcasted_iota(jnp.int32, (128, 128), 0) <= lax.broadcasted_iota(jnp.int32, (128, 128), 1)
    ).astype(F32).astype(BF)
    which = lax.broadcasted_iota(jnp.int32, (N_REP, 128), 0)
    carry = jnp.zeros((N_REP, 1), F32)
    members, ranks, keepers = [], [], []
    for b in range(UNIQ // 128):
        own = keeper[:, b * 128 : (b + 1) * 128]
        member = (which == own).astype(F32)
        running = nn(member.astype(BF), upper) + carry
        carry = running[:, 127:128]
        members.append(member)
        keepers.append(own.astype(F32))
        ranks.append(jnp.sum(member * (running - 1.0), axis=0, keepdims=True))
    member = jnp.concatenate(members, axis=1)
    rank = jnp.concatenate(ranks, axis=1)
    row_high = lax.shift_right_logical(row, 4).astype(F32)
    row_low = jnp.bitwise_and(row, 15).astype(F32)
    digits = jnp.concatenate([member * row_high, member * row_low], axis=0).astype(BF)
    ranked = lax.broadcasted_iota(jnp.int32, (CAP, UNIQ), 0).astype(F32) == rank
    where = nt(digits, ranked.astype(F32).astype(BF))
    wide = jnp.concatenate([where, jnp.zeros((2 * N_REP, 256 - CAP), F32)], axis=1)
    for k in range(N_REP):
        high, low = wide[k : k + 1, :], wide[N_REP + k : N_REP + k + 1, :]
        block = [high[:, 0:128], high[:, 128:256], low[:, 0:128], low[:, 128:256]]
        pos_ref[k] = jnp.concatenate(block + [jnp.zeros((12, 128), F32)], axis=0).astype(BF)
    table = jnp.concatenate(ranks + keepers, axis=0).astype(BF)
    found = []
    for p in range(2):
        slot = slot_ref[p : p + 1, :]
        low = jnp.bitwise_and(slot, 127)
        high = lax.shift_right_logical(slot, 7)
        hot_low = (lax.broadcasted_iota(jnp.int32, (128, SAMP), 0) == low).astype(F32).astype(BF)
        picked = nn(table, hot_low)
        hot_high = (lax.broadcasted_iota(jnp.int32, (16, SAMP), 0) == high).astype(F32)
        found.append(
            (
                jnp.sum(hot_high * picked[0:16, :], axis=0, keepdims=True),
                jnp.sum(hot_high * picked[16:32, :], axis=0, keepdims=True),
            )
        )
    rows = [row for pair in found for row in pair]
    found_ref[...] = jnp.concatenate(rows + [jnp.zeros((4, SAMP), F32)], axis=0)


def rows_kernel(found_ref, got_ref, pos_ref, _, out_hbm, hot, out_ref, sems):
    places = lax.broadcasted_iota(jnp.int32, (CAP, SAMP), 0).astype(F32).astype(BF)
    one, zero = jnp.ones((CAP, SAMP), BF), jnp.zeros((CAP, SAMP), BF)
    stores = []
    for j in range(4):
        for i in range(4):
            k = j * 4 + i
            hits = []
            for p in range(2):
                at, kept = found_ref[2 * p : 2 * p + 1, :], found_ref[2 * p + 1 : 2 * p + 2, :]
                own = jnp.where(kept == float(k), at, -1.0).astype(BF)
                hits.append(jnp.where(places == own, one, zero))
            hot[j % 2, i * CAP : (i + 1) * CAP, :] = hits[0] + hits[1]
        sums = nn(hot[j % 2], got_ref[...]).astype(BF)
        for i in range(4):
            k = j * 4 + i
            out_ref[k, 0:CAP, :] = sums[i * CAP : (i + 1) * CAP, :]
            out_ref[k, CAP:PAYLOAD, :] = pos_ref[k]
        some = slice(j * 4, j * 4 + 4)
        store = pltpu.make_async_copy(out_ref.at[some], out_hbm.at[some], sems.at[j])
        store.start()
        stores.append(store)
    for store in stores:
        store.wait()


def keep_kernel(got_ref, out_ref):
    names = lax.broadcasted_iota(jnp.int32, (KEEP, CAP), 0).astype(F32)
    acc = jnp.zeros((KEEP, EMB), F32)
    for g in range(N_REP):
        pos = got_ref[g, CAP:PAYLOAD, :].astype(F32)
        at = pos[0:2, :] * 16.0 + pos[2:4, :]
        at = jnp.concatenate([at[0:1, :], at[1:2, 0 : CAP - 128]], axis=1)
        hot = (names == at).astype(F32).astype(BF)
        acc = acc + nn(hot, got_ref[g, 0:CAP, :])
    out_ref[...] = acc


def call(kernel, outs, ins, scratch=(), mib=24, spare=None, us=2):
    return pl.pallas_call(
        kernel,
        out_shape=tuple(jax.ShapeDtypeStruct(s, d) for _, s, d in outs),
        in_specs=[spec for spec, _ in ins],
        out_specs=tuple(spec for spec, _, _ in outs),
        scratch_shapes=list(scratch),
        input_output_aliases={} if spare is None else {spare[0]: spare[1]},
        compiler_params=params(mib),
        cost_estimate=pl.CostEstimate(flops=us * 10**9, bytes_accessed=us * 10**6, transcendentals=0),
    )(*[a for _, a in ins])


def near(*arrays):
    return [(VMEM, a) for a in arrays]


def shifted(messages, axis):
    return [
        lax.ppermute(m, axis, [(i, (i + s) % 4) for i in range(4)]) for s, m in enumerate(messages, 1)
    ]


def shards(dense, pooled, cot, proj_v, proj_u, bias, lookup_slot, uniq_rows):
    place = (SMEM, lax.axis_index(REP + TABLE).astype(jnp.int32).reshape(1))
    swap = [(0, 1), (1, 0)]
    other = [lax.ppermute(a, "c", swap) for a in (dense, pooled, cot)]
    dma = pltpu.SemaphoreType.DMA
    dense2, pooled2, cot2 = other
    found, pos = call(
        index_kernel,
        [(VMEM, (8, SAMP), F32), (VMEM, (N_REP, 16, 128), BF)],
        near(uniq_rows.reshape(1, UNIQ), lookup_slot.reshape(SAMP, 2).T),
        mib=56,
    )
    u_shape, v_shape, lat_shape = (288, LAT), (544, LAT), (128, LAT)
    u0, u1, u2, u3, v_keep, v_send, latent, grad_latent = call(
        weight_kernel,
        [(HBM, u_shape, BF)] * 4 + [(HBM, v_shape, BF)] * 2 + [(VMEM, lat_shape, BF)] * 2,
        [place] + [(HBM, a) for a in (pooled, pooled2, dense, dense2, proj_v, cot, cot2, proj_u)]
        + [(ANY, found)],
        [pltpu.VMEM((256, w), BF) for w in (D0 - EMB, EMB, D0, D0)]
        + [pltpu.VMEM((D0, LAT), BF), pltpu.VMEM((LAT, D0), BF)]
        + [pltpu.VMEM((D0, LAT), F32), pltpu.VMEM((D0, LAT), F32), pltpu.VMEM((1, D0), F32)]
        + [pltpu.VMEM(u_shape, BF)] * 4
        + [pltpu.VMEM(v_shape, BF)] * 2
        + [dma((8,)), dma((6,))],
        mib=56,
        us=6,
    )
    bias_rows, out_shape = (D0 // 128, 128), (N_TAB, 128, EMB)
    (outgoing,) = call(
        pooled_kernel,
        [(HBM, out_shape, BF)],
        near(latent, grad_latent)
        + [(HBM, a) for a in (cot, proj_v, proj_u, bias.reshape(bias_rows))],
        [pltpu.VMEM((128, D0), BF), pltpu.VMEM((D0, LAT), BF), pltpu.VMEM((LAT, D0), BF)]
        + [pltpu.VMEM(bias_rows, F32), pltpu.VMEM(out_shape, BF)]
        + [dma((2,)), dma((4,)), dma((4,)), dma((4,))],
        mib=56,
        us=4,
    )
    received = lax.all_to_all(outgoing, TABLE, 0, 0, tiled=True).reshape(SAMP, EMB)
    u_got = shifted([u1, u2, u3], "y")
    v_got = lax.ppermute(v_send, "zl", swap)
    u_shape, v_shape = (160, LAT), (144, LAT)
    u_keep, u_send, v0, v1, v2, v3 = call(
        first_sum_kernel,
        [(VMEM, u_shape, F32), (HBM, u_shape, BF), (VMEM, v_shape, F32)] + [(HBM, v_shape, BF)] * 3,
        [place] + near(u0, *u_got, v_keep, v_got),
        [pltpu.VMEM((288, LAT), F32), pltpu.VMEM((544, LAT), F32), pltpu.VMEM(u_shape, BF)]
        + [pltpu.VMEM(v_shape, BF)] * 3
        + [dma((4,))],
        us=100,
    )
    (payload,) = call(
        rows_kernel,
        [(HBM, (N_REP, PAYLOAD, EMB), BF)],
        near(found, received, pos) + [(ANY, u_keep)],
        [pltpu.VMEM((2, 4 * CAP, SAMP), BF), pltpu.VMEM((N_REP, PAYLOAD, EMB), BF), dma((4,))],
        us=7,
    )
    u_got = lax.ppermute(u_send, "zl", swap)
    v_got = shifted([v1, v2, v3], "y")
    flat = [(0, 1), (1, 0), (2, 3), (3, 2)]
    cross = [(0, 3), (3, 0), (1, 2), (2, 1)]

    def halve(kernel, ins, in_rows, rows, axis, pairs, us=2, after=()):
        kept, sent = call(
            kernel,
            [(VMEM, (rows, LAT), F32), (HBM, (rows, LAT), BF)],
            [place] + near(*ins) + [(ANY, a) for a in after],
            [pltpu.VMEM((in_rows, LAT), F32), pltpu.VMEM((rows, LAT), BF), dma((1,))],
            us=us,
        )
        return kept, lax.ppermute(sent, axis, pairs)

    both = halve(second_sum_kernel, (u_keep, u_got, v0, *v_got), LAT, 208, "zh", flat, after=(payload,))
    gathered = lax.all_to_all(payload, REP, 0, 0, tiled=True)
    both = halve(third_sum_kernel, both, 208, 112, "x", flat, us=100)
    both = halve(fourth_sum_kernel, both, 112, 64, "x", cross)
    both = halve(fifth_sum_kernel, both, 64, 48, "zh", cross)
    part_u, part_v, whole_bias = call(
        last_kernel,
        [(VMEM, (LATP, FEAT), F32), (VMEM, (LATP, FEAT), F32), (VMEM, (D0 // 128, 128), F32)],
        near(*both),
    )
    (row_part,) = call(keep_kernel, [(VMEM, (KEEP, EMB), F32)], near(gathered))
    return part_u, part_v.T, whole_bias.reshape(D0), row_part.reshape(1, KEEP, EMB)


def solution(mesh):
    fine = Mesh(np.asarray(mesh.devices).reshape(4, 4, 2, 4, 2), ("zh", "x", "zl", "y", "c"))
    every = P(REP + TABLE, None)
    placed = (every, every, every, P(), P(), P(), P(REP, TABLE, None), P(REP, TABLE, None))
    return jax.shard_map(
        shards,
        mesh=fine,
        in_specs=placed,
        out_specs=(P(REP, TABLE), P(TABLE, REP), P(), P(TABLE, REP, None)),
        check_vma=False,
    )
```

```python
import jax
import jax.numpy as jnp
import numpy as np
from jax import lax
from jax.experimental import pallas as pl
from jax.experimental.pallas import tpu as pltpu
from jax.sharding import Mesh, PartitionSpec as P

BF = jnp.bfloat16
F32 = jnp.float32
TABLE = ("zl", "y", "c")
REP = ("zh", "x")
EMB = 128
LAT = 384
N_TAB = 16
N_REP = 16
D0 = 2176
FEAT = 136
LATP = 24
KEEP = 512
CAP = 160
SLOTS = N_REP * CAP
PAYLOAD = CAP + 16
UNIQ = 2048
SAMP = 2048
SCALE = float(32768) ** -0.5

HBM = pl.BlockSpec(memory_space=pltpu.HBM)
ANY = pl.BlockSpec(memory_space=pl.ANY)
VMEM = pl.BlockSpec(memory_space=pltpu.VMEM)
SMEM = pl.BlockSpec(memory_space=pltpu.SMEM)


def params(mib):
    return pltpu.CompilerParams(vmem_limit_bytes=mib * 1024 * 1024)


def coords(place_ref):
    i = place_ref[0]
    return (
        lax.shift_right_logical(i, 6),
        jnp.bitwise_and(lax.shift_right_logical(i, 4), 3),
        jnp.bitwise_and(lax.shift_right_logical(i, 3), 1),
        jnp.bitwise_and(lax.shift_right_logical(i, 1), 3),
        jnp.bitwise_and(i, 1),
    )


def nn(a, b):
    return lax.dot_general(a, b, (((1,), (0,)), ((), ())), preferred_element_type=F32)


def nt(a, b):
    return lax.dot_general(a, b, (((1,), (1,)), ((), ())), preferred_element_type=F32)


def tn(a, b):
    return lax.dot_general(a, b, (((0,), (0,)), ((), ())), preferred_element_type=F32)


def times(a, b):
    return (a.astype(F32) * b.astype(F32)).astype(BF)


def weight_kernel(
    place_ref, pooled_hbm, pooled2_hbm, dense_hbm, dense2_hbm, v_hbm, cot_hbm, cot2_hbm, u_hbm, bias_hbm, _,
    u0, u1, u2, u3, v_keep, v_send, out_hbm,
    pooled_ref, dense_ref, cot_ref, mix_ref, v_ref, u_ref,
    gu, gv, bias_row, bu0, bu1, bu2, bu3, bk, bs, bias_ref, out_ref, load_sems, sems, out_sems,
):
    own, other = slice(0, 128), slice(128, 256)
    pairs = (
        (pooled_hbm, pooled_ref.at[own, :]), (pooled2_hbm, pooled_ref.at[other, :]),
        (dense_hbm, dense_ref.at[own, :]), (dense2_hbm, dense_ref.at[other, :]),
        (v_hbm, v_ref), (cot_hbm, cot_ref.at[own, :]), (cot2_hbm, cot_ref.at[other, :]), (u_hbm, u_ref),
        (bias_hbm, bias_ref),
    )
    loads = [pltpu.make_async_copy(src, dst, load_sems.at[i]) for i, (src, dst) in enumerate(pairs)]
    for load in loads:
        load.start()
    for load in loads[:5]:
        load.wait()
    lat = (nn(dense_ref[...], v_ref[:EMB, :]) + nn(pooled_ref[...], v_ref[EMB:, :])).astype(BF)
    for load in loads[5:7]:
        load.wait()
    mix_ref[:, :EMB] = times(cot_ref[:, :EMB], dense_ref[...])
    mix_ref[:, EMB:] = times(cot_ref[:, EMB:], pooled_ref[...])
    for load in loads[7:]:
        load.wait()
    gl = nt(mix_ref[...], u_ref[...]).astype(BF)
    for j in range(D0 // EMB):
        cols = slice(j * EMB, (j + 1) * EMB)
        mix = mix_ref[:, cols]
        feat = dense_ref[...] if j == 0 else pooled_ref[:, (j - 1) * EMB : j * EMB]
        gu[cols, :] = tn(mix, lat)
        gv[cols, :] = tn(feat, gl)
        bias_row[:, cols] = jnp.sum(mix.astype(F32), axis=0, keepdims=True)
    high = bias_row[...].astype(BF)
    low = (bias_row[...] - high.astype(F32)).astype(BF)
    tail = jnp.zeros((1, 6 * LAT - D0), BF)
    rows = []
    for part in (high, low):
        whole = jnp.concatenate([part, tail], axis=1)
        rows += [whole[:, k * LAT : (k + 1) * LAT].astype(F32) for k in range(6)]
    rows.append(jnp.zeros((4, LAT), F32))
    bias_block = jnp.concatenate(rows, axis=0).astype(BF)
    _, _, zl, y, c = coords(place_ref)
    copies = []

    def block(g, zl, y):
        start = pl.multiple_of((zl * 8 + y * 2 + c) * FEAT, 8)
        return g[pl.ds(start, FEAT), :]

    def leave(buffer, out):
        copy = pltpu.make_async_copy(buffer, out, sems.at[len(copies)])
        copy.start()
        copies.append(copy)

    for s, (buffer, out) in enumerate(((bu0, u0), (bu1, u1), (bu2, u2), (bu3, u3))):
        dest_y = lax.rem(y + s, 4)
        buffer[0:272, :] = jnp.concatenate([block(gu, 0, dest_y), block(gu, 1, dest_y)], axis=0).astype(BF)
        buffer[272:288, :] = bias_block
        leave(buffer, out)
    for half, buffer, out in ((zl, bk, v_keep), (1 - zl, bs, v_send)):
        for i in range(2):
            pair = jnp.concatenate([block(gv, half, 2 * i), block(gv, half, 2 * i + 1)], axis=0)
            buffer[i * 272 : (i + 1) * 272, :] = pair.astype(BF)
        leave(buffer, out)
    latent, grad_latent = lat[0:128, :], gl[0:128, :]
    for t in range(N_TAB):
        cols = slice(EMB + t * EMB, EMB + (t + 1) * EMB)
        mixing = nn(latent, u_ref[:, cols]) + bias_ref[t + 1 : t + 2, :]
        backward = nt(grad_latent, v_ref[cols, :])
        out_ref[t] = (cot_ref[0:128, cols].astype(F32) * (mixing + 1.0) + backward).astype(BF)
        if t % 4 == 3:
            some = slice(t - 3, t + 1)
            copy = pltpu.make_async_copy(out_ref.at[some], out_hbm.at[some], out_sems.at[t // 4])
            copy.start()
            copies.append(copy)
    for copy in copies:
        copy.wait()


def bias_again(block):
    total = block[0:6, :] + block[6:12, :]
    high = total.astype(BF).astype(F32)
    low = (total - high).astype(BF).astype(F32)
    return jnp.concatenate([high, low, jnp.zeros((4, LAT), F32)], axis=0)


def first_u_kernel(place_ref, m0, m1, m2, m3, _, keep_ref, send_ref, acc, buffer, sem):
    acc[...] = (m0[...].astype(F32) + m1[...].astype(F32)) + (m2[...].astype(F32) + m3[...].astype(F32))
    _, _, zl, _, _ = coords(place_ref)
    rest = [jnp.zeros((8, LAT), F32), bias_again(acc[272:288, :])]
    kept = pick(acc, [zl * FEAT], FEAT) + rest
    split(keep_ref, send_ref, buffer, sem, kept, pick(acc, [(1 - zl) * FEAT], FEAT) + rest)


def first_v_kernel(place_ref, own, got, v0, v1, v2, v3, acc, b1, b2, b3, sems):
    acc[...] = own[...].astype(F32) + got[...].astype(F32)
    _, _, _, y, _ = coords(place_ref)
    gap = [jnp.zeros((8, LAT), F32)]
    copies = []
    for s, buffer, out in ((1, b1, v1), (2, b2, v2), (3, b3, v3)):
        block = pick(acc, [lax.rem(y + s, 4) * FEAT], FEAT)
        buffer[...] = jnp.concatenate(block + gap, axis=0).astype(BF)
        copy = pltpu.make_async_copy(buffer, out, sems.at[s])
        copy.start()
        copies.append(copy)
    v0[...] = jnp.concatenate(pick(acc, [y * FEAT], FEAT) + gap, axis=0)
    for copy in copies:
        copy.wait()


def pick(ref, starts, rows):
    return [ref[pl.ds(pl.multiple_of(start, 8), rows), :] for start in starts]


def split(keep_ref, send_ref, buffer, sem, kept, sent):
    buffer[...] = jnp.concatenate(sent, axis=0).astype(BF)
    copy = pltpu.make_async_copy(buffer, send_ref, sem.at[0])
    copy.start()
    keep_ref[...] = jnp.concatenate(kept, axis=0)
    copy.wait()


def second_sum_kernel(
    place_ref, u_keep, u_got, v0, v1, v2, v3, _, keep_ref, send_ref, flip, buffer, sem
):
    u = u_keep[...] + u_got[...].astype(F32)
    v = (v0[...] + v1[...].astype(F32)) + (v2[...].astype(F32) + v3[...].astype(F32))
    bias = bias_again(u[144:160, :])
    stacked = jnp.concatenate(
        [u[0:128], v[0:128], u[128:136], v[128:136], jnp.zeros((112, LAT), F32)], axis=0
    )
    flip[...] = stacked.T
    zh, x, _, _, _ = coords(place_ref)

    def rows_of(dest):
        order = (x, 3 - x, jnp.bitwise_xor(x, 1), jnp.bitwise_xor(x, 2))
        return pick(flip, [(dest * 4 + dest_x) * LATP for dest_x in order], LATP)

    kept = rows_of(zh) + rows_of(3 - zh) + [bias]
    sent = rows_of(jnp.bitwise_xor(zh, 1)) + rows_of(jnp.bitwise_xor(zh, 2)) + [bias]
    split(keep_ref, send_ref, buffer, sem, kept, sent)


def third_sum_kernel(_, keep, got, keep_ref, send_ref, acc, buffer, sem):
    acc[...] = keep[...] + got[...].astype(F32)
    bias = bias_again(acc[192:208, :])
    kept = [acc[0:48, :], acc[96:144, :], bias]
    split(keep_ref, send_ref, buffer, sem, kept, [acc[48:96, :], acc[144:192, :], bias])


def fourth_sum_kernel(_, keep, got, keep_ref, send_ref, acc, buffer, sem):
    acc[...] = keep[...] + got[...].astype(F32)
    bias = bias_again(acc[96:112, :])
    kept = [acc[0:24, :], acc[48:72, :], bias]
    split(keep_ref, send_ref, buffer, sem, kept, [acc[24:48, :], acc[72:96, :], bias])


def fifth_sum_kernel(_, keep, got, keep_ref, send_ref, acc, buffer, sem):
    acc[...] = keep[...] + got[...].astype(F32)
    bias = bias_again(acc[48:64, :])
    gap = jnp.zeros((8, LAT), F32)
    split(keep_ref, send_ref, buffer, sem, [acc[0:24, :], gap, bias], [acc[24:48, :], gap, bias])


def last_kernel(keep, got, u_ref, v_ref, bias_ref):
    total = keep[...] + got[...].astype(F32)
    total = total * SCALE
    u_ref[:, 0:128] = total[0:LATP, 0:128]
    u_ref[:, 128:136] = total[0:LATP, 256:264]
    v_ref[:, 0:128] = total[0:LATP, 128:256]
    v_ref[:, 128:136] = total[0:LATP, 264:272]
    bias = total[32:38, :] + total[38:44, :]
    for j in range(D0 // 128):
        k, at = j // 3, (j % 3) * 128
        bias_ref[j : j + 1, :] = bias[k : k + 1, at : at + 128]


def index_kernel(uniq_ref, slot_ref, found_ref, pos_ref):
    uniq = uniq_ref[...]
    keeper = lax.shift_right_logical(uniq, 9)
    row = jnp.bitwise_and(uniq, KEEP - 1)
    upper = (
        lax.broadcasted_iota(jnp.int32, (128, 128), 0) <= lax.broadcasted_iota(jnp.int32, (128, 128), 1)
    ).astype(F32).astype(BF)
    which = lax.broadcasted_iota(jnp.int32, (N_REP, 128), 0)
    carry = jnp.zeros((N_REP, 1), F32)
    members, ranks, keepers = [], [], []
    for b in range(UNIQ // 128):
        own = keeper[:, b * 128 : (b + 1) * 128]
        member = (which == own).astype(F32)
        running = nn(member.astype(BF), upper) + carry
        carry = running[:, 127:128]
        members.append(member)
        keepers.append(own.astype(F32))
        ranks.append(jnp.sum(member * (running - 1.0), axis=0, keepdims=True))
    member = jnp.concatenate(members, axis=1)
    rank = jnp.concatenate(ranks, axis=1)
    row_high = lax.shift_right_logical(row, 4).astype(F32)
    row_low = jnp.bitwise_and(row, 15).astype(F32)
    digits = jnp.concatenate([member * row_high, member * row_low], axis=0).astype(BF)
    ranked = lax.broadcasted_iota(jnp.int32, (CAP, UNIQ), 0).astype(F32) == rank
    where = nt(digits, ranked.astype(F32).astype(BF))
    wide = jnp.concatenate([where, jnp.zeros((2 * N_REP, 256 - CAP), F32)], axis=1)
    for k in range(N_REP):
        high, low = wide[k : k + 1, :], wide[N_REP + k : N_REP + k + 1, :]
        block = [high[:, 0:128], high[:, 128:256], low[:, 0:128], low[:, 128:256]]
        pos_ref[k] = jnp.concatenate(block + [jnp.zeros((12, 128), F32)], axis=0).astype(BF)
    table = jnp.concatenate(ranks + keepers, axis=0).astype(BF)
    found = []
    for p in range(2):
        slot = slot_ref[p : p + 1, :]
        low = jnp.bitwise_and(slot, 127)
        high = lax.shift_right_logical(slot, 7)
        hot_low = (lax.broadcasted_iota(jnp.int32, (128, SAMP), 0) == low).astype(F32).astype(BF)
        picked = nn(table, hot_low)
        hot_high = (lax.broadcasted_iota(jnp.int32, (16, SAMP), 0) == high).astype(F32)
        found.append(
            (
                jnp.sum(hot_high * picked[0:16, :], axis=0, keepdims=True),
                jnp.sum(hot_high * picked[16:32, :], axis=0, keepdims=True),
            )
        )
    rows = [row for pair in found for row in pair]
    found_ref[...] = jnp.concatenate(rows + [jnp.zeros((4, SAMP), F32)], axis=0)


def rows_kernel(found_ref, got_ref, pos_ref, _, out_hbm, hot, out_ref, sems):
    places = lax.broadcasted_iota(jnp.int32, (CAP, SAMP), 0).astype(F32).astype(BF)
    one, zero = jnp.ones((CAP, SAMP), BF), jnp.zeros((CAP, SAMP), BF)
    stores = []
    for j in range(4):
        for i in range(4):
            k = j * 4 + i
            hits = []
            for p in range(2):
                at, kept = found_ref[2 * p : 2 * p + 1, :], found_ref[2 * p + 1 : 2 * p + 2, :]
                own = jnp.where(kept == float(k), at, -1.0).astype(BF)
                hits.append(jnp.where(places == own, one, zero))
            hot[j % 2, i * CAP : (i + 1) * CAP, :] = hits[0] + hits[1]
        sums = nn(hot[j % 2], got_ref[...]).astype(BF)
        for i in range(4):
            k = j * 4 + i
            out_ref[k, 0:CAP, :] = sums[i * CAP : (i + 1) * CAP, :]
            out_ref[k, CAP:PAYLOAD, :] = pos_ref[k]
        some = slice(j * 4, j * 4 + 4)
        store = pltpu.make_async_copy(out_ref.at[some], out_hbm.at[some], sems.at[j])
        store.start()
        stores.append(store)
    for store in stores:
        store.wait()


def keep_kernel(got_ref, out_ref):
    names = lax.broadcasted_iota(jnp.int32, (KEEP, CAP), 0).astype(F32)
    acc = jnp.zeros((KEEP, EMB), F32)
    for g in range(N_REP):
        pos = got_ref[g, CAP:PAYLOAD, :].astype(F32)
        at = pos[0:2, :] * 16.0 + pos[2:4, :]
        at = jnp.concatenate([at[0:1, :], at[1:2, 0 : CAP - 128]], axis=1)
        hot = (names == at).astype(F32).astype(BF)
        acc = acc + nn(hot, got_ref[g, 0:CAP, :])
    out_ref[...] = acc


def call(kernel, outs, ins, scratch=(), mib=24, spare=None, us=2):
    return pl.pallas_call(
        kernel,
        out_shape=tuple(jax.ShapeDtypeStruct(s, d) for _, s, d in outs),
        in_specs=[spec for spec, _ in ins],
        out_specs=tuple(spec for spec, _, _ in outs),
        scratch_shapes=list(scratch),
        input_output_aliases={} if spare is None else {spare[0]: spare[1]},
        compiler_params=params(mib),
        cost_estimate=pl.CostEstimate(flops=us * 10**9, bytes_accessed=us * 10**6, transcendentals=0),
    )(*[a for _, a in ins])


def near(*arrays):
    return [(VMEM, a) for a in arrays]


def shifted(messages, axis):
    return [
        lax.ppermute(m, axis, [(i, (i + s) % 4) for i in range(4)]) for s, m in enumerate(messages, 1)
    ]


def shards(dense, pooled, cot, proj_v, proj_u, bias, lookup_slot, uniq_rows):
    place = (SMEM, lax.axis_index(REP + TABLE).astype(jnp.int32).reshape(1))
    swap = [(0, 1), (1, 0)]
    other = [lax.ppermute(a, "c", swap) for a in (dense, pooled, cot)]
    dma = pltpu.SemaphoreType.DMA
    dense2, pooled2, cot2 = other
    found, pos = call(
        index_kernel,
        [(VMEM, (8, SAMP), F32), (VMEM, (N_REP, 16, 128), BF)],
        near(uniq_rows.reshape(1, UNIQ), lookup_slot.reshape(SAMP, 2).T),
        mib=56,
    )
    u_shape, v_shape = (288, LAT), (544, LAT)
    bias_rows, out_shape = (D0 // 128, 128), (N_TAB, 128, EMB)
    loaded = (pooled, pooled2, dense, dense2, proj_v, cot, cot2, proj_u, bias.reshape(bias_rows))
    u0, u1, u2, u3, v_keep, v_send, outgoing = call(
        weight_kernel,
        [(HBM, u_shape, BF)] * 4 + [(HBM, v_shape, BF)] * 2 + [(HBM, out_shape, BF)],
        [place] + [(HBM, a) for a in loaded] + [(ANY, found)],
        [pltpu.VMEM((256, w), BF) for w in (D0 - EMB, EMB, D0, D0)]
        + [pltpu.VMEM((D0, LAT), BF), pltpu.VMEM((LAT, D0), BF)]
        + [pltpu.VMEM((D0, LAT), F32), pltpu.VMEM((D0, LAT), F32), pltpu.VMEM((1, D0), F32)]
        + [pltpu.VMEM(u_shape, BF)] * 4
        + [pltpu.VMEM(v_shape, BF)] * 2
        + [pltpu.VMEM(bias_rows, F32), pltpu.VMEM(out_shape, BF)]
        + [dma((9,)), dma((6,)), dma((4,))],
        mib=56,
        us=8,
    )
    received = lax.all_to_all(outgoing, TABLE, 0, 0, tiled=True).reshape(SAMP, EMB)
    u_got = shifted([u1, u2, u3], "y")
    v_got = lax.ppermute(v_send, "zl", swap)
    u_shape, v_shape = (160, LAT), (144, LAT)
    v0, v1, v2, v3 = call(
        first_v_kernel,
        [(VMEM, v_shape, F32)] + [(HBM, v_shape, BF)] * 3,
        [place] + near(v_keep, v_got),
        [pltpu.VMEM((544, LAT), F32)] + [pltpu.VMEM(v_shape, BF)] * 3 + [dma((4,))],
        us=2,
    )
    v_got = shifted([v1, v2, v3], "y")
    u_keep, u_send = call(
        first_u_kernel,
        [(VMEM, u_shape, F32), (HBM, u_shape, BF)],
        [place] + near(u0, *u_got) + [(ANY, v0)],
        [pltpu.VMEM((288, LAT), F32), pltpu.VMEM(u_shape, BF), dma((1,))],
        us=100,
    )
    (payload,) = call(
        rows_kernel,
        [(HBM, (N_REP, PAYLOAD, EMB), BF)],
        near(found, received, pos) + [(ANY, u_keep)],
        [pltpu.VMEM((2, 4 * CAP, SAMP), BF), pltpu.VMEM((N_REP, PAYLOAD, EMB), BF), dma((4,))],
        us=7,
    )
    u_got = lax.ppermute(u_send, "zl", swap)
    flat = [(0, 1), (1, 0), (2, 3), (3, 2)]
    cross = [(0, 3), (3, 0), (1, 2), (2, 1)]

    def halve(kernel, ins, in_rows, rows, axis, pairs, us=2, after=()):
        kept, sent = call(
            kernel,
            [(VMEM, (rows, LAT), F32), (HBM, (rows, LAT), BF)],
            [place] + near(*ins) + [(ANY, a) for a in after],
            [pltpu.VMEM((in_rows, LAT), F32), pltpu.VMEM((rows, LAT), BF), dma((1,))],
            us=us,
        )
        return kept, lax.ppermute(sent, axis, pairs)

    both = halve(second_sum_kernel, (u_keep, u_got, v0, *v_got), LAT, 208, "zh", flat, after=(payload,))
    gathered = lax.all_to_all(payload, REP, 0, 0, tiled=True)
    both = halve(third_sum_kernel, both, 208, 112, "x", flat, us=100)
    both = halve(fourth_sum_kernel, both, 112, 64, "x", cross)
    both = halve(fifth_sum_kernel, both, 64, 48, "zh", cross)
    part_u, part_v, whole_bias = call(
        last_kernel,
        [(VMEM, (LATP, FEAT), F32), (VMEM, (LATP, FEAT), F32), (VMEM, (D0 // 128, 128), F32)],
        near(*both),
    )
    (row_part,) = call(keep_kernel, [(VMEM, (KEEP, EMB), F32)], near(gathered))
    return part_u, part_v.T, whole_bias.reshape(D0), row_part.reshape(1, KEEP, EMB)


def solution(mesh):
    fine = Mesh(np.asarray(mesh.devices).reshape(4, 4, 2, 4, 2), ("zh", "x", "zl", "y", "c"))
    every = P(REP + TABLE, None)
    placed = (every, every, every, P(), P(), P(), P(REP, TABLE, None), P(REP, TABLE, None))
    return jax.shard_map(
        shards,
        mesh=fine,
        in_specs=placed,
        out_specs=(P(REP, TABLE), P(TABLE, REP), P(), P(TABLE, REP, None)),
        check_vma=False,
    )
```

```python
import jax
import jax.numpy as jnp
import numpy as np
from jax import lax
from jax.experimental import pallas as pl
from jax.experimental.pallas import tpu as pltpu
from jax.sharding import Mesh, PartitionSpec as P

BF = jnp.bfloat16
F32 = jnp.float32
TABLE = ("zl", "y", "c")
REP = ("zh", "x")
EMB = 128
LAT = 384
N_TAB = 16
N_REP = 16
D0 = 2176
FEAT = 136
LATP = 24
KEEP = 512
CAP = 160
SLOTS = N_REP * CAP
PAYLOAD = CAP + 16
UNIQ = 2048
SAMP = 2048
SCALE = float(32768) ** -0.5

HBM = pl.BlockSpec(memory_space=pltpu.HBM)
ANY = pl.BlockSpec(memory_space=pl.ANY)
VMEM = pl.BlockSpec(memory_space=pltpu.VMEM)
SMEM = pl.BlockSpec(memory_space=pltpu.SMEM)


def params(mib):
    return pltpu.CompilerParams(vmem_limit_bytes=mib * 1024 * 1024)


def coords(place_ref):
    i = place_ref[0]
    return (
        lax.shift_right_logical(i, 6),
        jnp.bitwise_and(lax.shift_right_logical(i, 4), 3),
        jnp.bitwise_and(lax.shift_right_logical(i, 3), 1),
        jnp.bitwise_and(lax.shift_right_logical(i, 1), 3),
        jnp.bitwise_and(i, 1),
    )


def nn(a, b):
    return lax.dot_general(a, b, (((1,), (0,)), ((), ())), preferred_element_type=F32)


def nt(a, b):
    return lax.dot_general(a, b, (((1,), (1,)), ((), ())), preferred_element_type=F32)


def tn(a, b):
    return lax.dot_general(a, b, (((0,), (0,)), ((), ())), preferred_element_type=F32)


def times(a, b):
    return (a.astype(F32) * b.astype(F32)).astype(BF)


def weight_kernel(
    place_ref, pooled_hbm, pooled2_hbm, dense_hbm, dense2_hbm, v_hbm, cot_hbm, cot2_hbm, u_hbm, bias_hbm,
    u0, u1, u2, u3, v_keep, v_send, out_hbm,
    pooled_ref, dense_ref, cot_ref, mix_ref, v_ref, u_ref,
    gu, gv, bias_row, bu0, bu1, bu2, bu3, bk, bs, bias_ref, out_ref, load_sems, sems, out_sems,
):
    own, other = slice(0, 128), slice(128, 256)
    pairs = (
        (pooled_hbm, pooled_ref.at[own, :]), (pooled2_hbm, pooled_ref.at[other, :]),
        (dense_hbm, dense_ref.at[own, :]), (dense2_hbm, dense_ref.at[other, :]),
        (v_hbm, v_ref), (cot_hbm, cot_ref.at[own, :]), (cot2_hbm, cot_ref.at[other, :]), (u_hbm, u_ref),
        (bias_hbm, bias_ref),
    )
    loads = [pltpu.make_async_copy(src, dst, load_sems.at[i]) for i, (src, dst) in enumerate(pairs)]
    for load in loads:
        load.start()
    for load in loads[:5]:
        load.wait()
    lat = (nn(dense_ref[...], v_ref[:EMB, :]) + nn(pooled_ref[...], v_ref[EMB:, :])).astype(BF)
    for load in loads[5:7]:
        load.wait()
    mix_ref[:, :EMB] = times(cot_ref[:, :EMB], dense_ref[...])
    mix_ref[:, EMB:] = times(cot_ref[:, EMB:], pooled_ref[...])
    for load in loads[7:]:
        load.wait()
    gl = nt(mix_ref[...], u_ref[...]).astype(BF)
    for j in range(D0 // EMB):
        cols = slice(j * EMB, (j + 1) * EMB)
        mix = mix_ref[:, cols]
        feat = dense_ref[...] if j == 0 else pooled_ref[:, (j - 1) * EMB : j * EMB]
        gu[cols, :] = tn(mix, lat)
        gv[cols, :] = tn(feat, gl)
        bias_row[:, cols] = jnp.sum(mix.astype(F32), axis=0, keepdims=True)
    high = bias_row[...].astype(BF)
    low = (bias_row[...] - high.astype(F32)).astype(BF)
    tail = jnp.zeros((1, 6 * LAT - D0), BF)
    rows = []
    for part in (high, low):
        whole = jnp.concatenate([part, tail], axis=1)
        rows += [whole[:, k * LAT : (k + 1) * LAT].astype(F32) for k in range(6)]
    rows.append(jnp.zeros((4, LAT), F32))
    bias_block = jnp.concatenate(rows, axis=0).astype(BF)
    _, _, zl, y, c = coords(place_ref)
    copies = []

    def block(g, zl, y):
        start = pl.multiple_of((zl * 8 + y * 2 + c) * FEAT, 8)
        return g[pl.ds(start, FEAT), :]

    def leave(buffer, out):
        copy = pltpu.make_async_copy(buffer, out, sems.at[len(copies)])
        copy.start()
        copies.append(copy)

    for s, (buffer, out) in enumerate(((bu0, u0), (bu1, u1), (bu2, u2), (bu3, u3))):
        dest_y = lax.rem(y + s, 4)
        buffer[0:272, :] = jnp.concatenate([block(gu, 0, dest_y), block(gu, 1, dest_y)], axis=0).astype(BF)
        buffer[272:288, :] = bias_block
        leave(buffer, out)
    for half, buffer, out in ((zl, bk, v_keep), (1 - zl, bs, v_send)):
        for i in range(2):
            pair = jnp.concatenate([block(gv, half, 2 * i), block(gv, half, 2 * i + 1)], axis=0)
            buffer[i * 272 : (i + 1) * 272, :] = pair.astype(BF)
        leave(buffer, out)
    latent, grad_latent = lat[0:128, :], gl[0:128, :]
    for t in range(N_TAB):
        cols = slice(EMB + t * EMB, EMB + (t + 1) * EMB)
        mixing = nn(latent, u_ref[:, cols]) + bias_ref[t + 1 : t + 2, :]
        backward = nt(grad_latent, v_ref[cols, :])
        out_ref[t] = (cot_ref[0:128, cols].astype(F32) * (mixing + 1.0) + backward).astype(BF)
        if t % 4 == 3:
            some = slice(t - 3, t + 1)
            copy = pltpu.make_async_copy(out_ref.at[some], out_hbm.at[some], out_sems.at[t // 4])
            copy.start()
            copies.append(copy)
    for copy in copies:
        copy.wait()


def bias_again(block):
    total = block[0:6, :] + block[6:12, :]
    high = total.astype(BF).astype(F32)
    low = (total - high).astype(BF).astype(F32)
    return jnp.concatenate([high, low, jnp.zeros((4, LAT), F32)], axis=0)


def first_u_kernel(place_ref, m0, m1, m2, m3, _, keep_ref, send_ref, acc, buffer, sem):
    acc[...] = (m0[...].astype(F32) + m1[...].astype(F32)) + (m2[...].astype(F32) + m3[...].astype(F32))
    _, _, zl, _, _ = coords(place_ref)
    rest = [jnp.zeros((8, LAT), F32), bias_again(acc[272:288, :])]
    kept = pick(acc, [zl * FEAT], FEAT) + rest
    split(keep_ref, send_ref, buffer, sem, kept, pick(acc, [(1 - zl) * FEAT], FEAT) + rest)


def first_v_kernel(place_ref, own, got, v0, v1, v2, v3, acc, b1, b2, b3, sems):
    acc[...] = own[...].astype(F32) + got[...].astype(F32)
    _, _, _, y, _ = coords(place_ref)
    gap = [jnp.zeros((8, LAT), F32)]
    copies = []
    for s, buffer, out in ((1, b1, v1), (2, b2, v2), (3, b3, v3)):
        block = pick(acc, [lax.rem(y + s, 4) * FEAT], FEAT)
        buffer[...] = jnp.concatenate(block + gap, axis=0).astype(BF)
        copy = pltpu.make_async_copy(buffer, out, sems.at[s])
        copy.start()
        copies.append(copy)
    v0[...] = jnp.concatenate(pick(acc, [y * FEAT], FEAT) + gap, axis=0)
    for copy in copies:
        copy.wait()


def pick(ref, starts, rows):
    return [ref[pl.ds(pl.multiple_of(start, 8), rows), :] for start in starts]


def split(keep_ref, send_ref, buffer, sem, kept, sent):
    buffer[...] = jnp.concatenate(sent, axis=0).astype(BF)
    copy = pltpu.make_async_copy(buffer, send_ref, sem.at[0])
    copy.start()
    keep_ref[...] = jnp.concatenate(kept, axis=0)
    copy.wait()


def second_sum_kernel(
    place_ref, u_keep, u_got, v0, v1, v2, v3, _, keep_ref, send_ref, flip, buffer, sem
):
    u = u_keep[...] + u_got[...].astype(F32)
    v = (v0[...] + v1[...].astype(F32)) + (v2[...].astype(F32) + v3[...].astype(F32))
    bias = bias_again(u[144:160, :])
    stacked = jnp.concatenate(
        [u[0:128], v[0:128], u[128:136], v[128:136], jnp.zeros((112, LAT), F32)], axis=0
    )
    flip[...] = stacked.T
    zh, x, _, _, _ = coords(place_ref)

    def rows_of(dest):
        order = (x, 3 - x, jnp.bitwise_xor(x, 1), jnp.bitwise_xor(x, 2))
        return pick(flip, [(dest * 4 + dest_x) * LATP for dest_x in order], LATP)

    kept = rows_of(zh) + rows_of(3 - zh) + [bias]
    sent = rows_of(jnp.bitwise_xor(zh, 1)) + rows_of(jnp.bitwise_xor(zh, 2)) + [bias]
    split(keep_ref, send_ref, buffer, sem, kept, sent)


def third_sum_kernel(_, keep, got, keep_ref, send_ref, acc, buffer, sem):
    acc[...] = keep[...] + got[...].astype(F32)
    bias = bias_again(acc[192:208, :])
    kept = [acc[0:48, :], acc[96:144, :], bias]
    split(keep_ref, send_ref, buffer, sem, kept, [acc[48:96, :], acc[144:192, :], bias])


def fourth_sum_kernel(_, keep, got, keep_ref, send_ref, acc, buffer, sem):
    acc[...] = keep[...] + got[...].astype(F32)
    bias = bias_again(acc[96:112, :])
    kept = [acc[0:24, :], acc[48:72, :], bias]
    split(keep_ref, send_ref, buffer, sem, kept, [acc[24:48, :], acc[72:96, :], bias])


def fifth_sum_kernel(_, keep, got, keep_ref, send_ref, acc, buffer, sem):
    acc[...] = keep[...] + got[...].astype(F32)
    bias = bias_again(acc[48:64, :])
    gap = jnp.zeros((8, LAT), F32)
    split(keep_ref, send_ref, buffer, sem, [acc[0:24, :], gap, bias], [acc[24:48, :], gap, bias])


def last_kernel(keep, got, u_ref, v_ref, bias_ref):
    total = keep[...] + got[...].astype(F32)
    total = total * SCALE
    u_ref[:, 0:128] = total[0:LATP, 0:128]
    u_ref[:, 128:136] = total[0:LATP, 256:264]
    v_ref[:, 0:128] = total[0:LATP, 128:256]
    v_ref[:, 128:136] = total[0:LATP, 264:272]
    bias = total[32:38, :] + total[38:44, :]
    for j in range(D0 // 128):
        k, at = j // 3, (j % 3) * 128
        bias_ref[j : j + 1, :] = bias[k : k + 1, at : at + 128]


def index_kernel(uniq_ref, slot_ref, _, found_ref, pos_ref):
    uniq = uniq_ref[...]
    keeper = lax.shift_right_logical(uniq, 9)
    row = jnp.bitwise_and(uniq, KEEP - 1)
    upper = (
        lax.broadcasted_iota(jnp.int32, (128, 128), 0) <= lax.broadcasted_iota(jnp.int32, (128, 128), 1)
    ).astype(F32).astype(BF)
    which = lax.broadcasted_iota(jnp.int32, (N_REP, 128), 0)
    carry = jnp.zeros((N_REP, 1), F32)
    members, ranks, keepers = [], [], []
    for b in range(UNIQ // 128):
        own = keeper[:, b * 128 : (b + 1) * 128]
        member = (which == own).astype(F32)
        running = nn(member.astype(BF), upper) + carry
        carry = running[:, 127:128]
        members.append(member)
        keepers.append(own.astype(F32))
        ranks.append(jnp.sum(member * (running - 1.0), axis=0, keepdims=True))
    member = jnp.concatenate(members, axis=1)
    rank = jnp.concatenate(ranks, axis=1)
    row_high = lax.shift_right_logical(row, 8).astype(F32)
    row_low = jnp.bitwise_and(row, 255).astype(F32)
    digits = jnp.concatenate([member * row_high, member * row_low], axis=0).astype(BF)
    ranked = lax.broadcasted_iota(jnp.int32, (CAP, UNIQ), 0).astype(F32) == rank
    where = nt(digits, ranked.astype(F32).astype(BF))
    wide = jnp.concatenate([where, jnp.zeros((2 * N_REP, 256 - CAP), F32)], axis=1)
    for k in range(N_REP):
        high, low = wide[k : k + 1, :], wide[N_REP + k : N_REP + k + 1, :]
        block = [high[:, 0:128], high[:, 128:256], low[:, 0:128], low[:, 128:256]]
        pos_ref[k] = jnp.concatenate(block + [jnp.zeros((12, 128), F32)], axis=0).astype(BF)
    table = jnp.concatenate(ranks + keepers, axis=0).astype(BF)
    found = []
    for p in range(2):
        slot = slot_ref[p : p + 1, :]
        low = jnp.bitwise_and(slot, 127)
        high = lax.shift_right_logical(slot, 7)
        hot_low = (lax.broadcasted_iota(jnp.int32, (128, SAMP), 0) == low).astype(F32).astype(BF)
        picked = nn(table, hot_low)
        hot_high = (lax.broadcasted_iota(jnp.int32, (16, SAMP), 0) == high).astype(F32)
        found.append(
            (
                jnp.sum(hot_high * picked[0:16, :], axis=0, keepdims=True),
                jnp.sum(hot_high * picked[16:32, :], axis=0, keepdims=True),
            )
        )
    rows = [row for pair in found for row in pair]
    found_ref[...] = jnp.concatenate(rows + [jnp.zeros((4, SAMP), F32)], axis=0)


def rows_kernel(found_ref, got_ref, pos_ref, _, out_hbm, hot, out_ref, sems):
    places = lax.broadcasted_iota(jnp.int32, (CAP, SAMP), 0).astype(F32).astype(BF)
    one, zero = jnp.ones((CAP, SAMP), BF), jnp.zeros((CAP, SAMP), BF)
    stores = []
    for j in range(4):
        for i in range(4):
            k = j * 4 + i
            hits = []
            for p in range(2):
                at, kept = found_ref[2 * p : 2 * p + 1, :], found_ref[2 * p + 1 : 2 * p + 2, :]
                own = jnp.where(kept == float(k), at, -1.0).astype(BF)
                hits.append(jnp.where(places == own, one, zero))
            hot[j % 2, i * CAP : (i + 1) * CAP, :] = hits[0] + hits[1]
        sums = nn(hot[j % 2], got_ref[...]).astype(BF)
        for i in range(4):
            k = j * 4 + i
            out_ref[k, 0:CAP, :] = sums[i * CAP : (i + 1) * CAP, :]
            out_ref[k, CAP:PAYLOAD, :] = pos_ref[k]
        some = slice(j * 4, j * 4 + 4)
        store = pltpu.make_async_copy(out_ref.at[some], out_hbm.at[some], sems.at[j])
        store.start()
        stores.append(store)
    for store in stores:
        store.wait()


def keep_kernel(got_ref, out_ref):
    names = lax.broadcasted_iota(jnp.int32, (256, CAP), 0).astype(F32).astype(BF)
    one, zero = jnp.ones((256, CAP), BF), jnp.zeros((256, CAP), BF)
    accs = [jnp.zeros((256, EMB), F32) for _ in range(2)]
    for g in range(N_REP):
        pos = got_ref[g, CAP:PAYLOAD, :].astype(F32)
        at = [jnp.concatenate([pos[i : i + 1, :], pos[i + 1 : i + 2, 0 : CAP - 128]], axis=1) for i in (0, 2)]
        for half in range(2):
            own = jnp.where(at[0] == float(half), at[1], -1.0).astype(BF)
            hot = jnp.where(names == own, one, zero)
            accs[half] = accs[half] + nn(hot, got_ref[g, 0:CAP, :])
    for half in range(2):
        out_ref[half * 256 : (half + 1) * 256, :] = accs[half]


def call(kernel, outs, ins, scratch=(), mib=24, spare=None, us=2):
    return pl.pallas_call(
        kernel,
        out_shape=tuple(jax.ShapeDtypeStruct(s, d) for _, s, d in outs),
        in_specs=[spec for spec, _ in ins],
        out_specs=tuple(spec for spec, _, _ in outs),
        scratch_shapes=list(scratch),
        input_output_aliases={} if spare is None else {spare[0]: spare[1]},
        compiler_params=params(mib),
        cost_estimate=pl.CostEstimate(flops=us * 10**9, bytes_accessed=us * 10**6, transcendentals=0),
    )(*[a for _, a in ins])


def near(*arrays):
    return [(VMEM, a) for a in arrays]


def shifted(messages, axis):
    got = {
        s: lax.ppermute(messages[s - 1], axis, [(i, (i + s) % 4) for i in range(4)]) for s in (2, 1, 3)
    }
    return [got[s] for s in (1, 2, 3)]


def shards(dense, pooled, cot, proj_v, proj_u, bias, lookup_slot, uniq_rows):
    place = (SMEM, lax.axis_index(REP + TABLE).astype(jnp.int32).reshape(1))
    swap = [(0, 1), (1, 0)]
    other = [lax.ppermute(a, "c", swap) for a in (dense, pooled, cot)]
    dma = pltpu.SemaphoreType.DMA
    dense2, pooled2, cot2 = other
    u_shape, v_shape = (288, LAT), (544, LAT)
    bias_rows, out_shape = (D0 // 128, 128), (N_TAB, 128, EMB)
    loaded = (pooled, pooled2, dense, dense2, proj_v, cot, cot2, proj_u, bias.reshape(bias_rows))
    u0, u1, u2, u3, v_keep, v_send, outgoing = call(
        weight_kernel,
        [(HBM, u_shape, BF)] * 4 + [(HBM, v_shape, BF)] * 2 + [(HBM, out_shape, BF)],
        [place] + [(HBM, a) for a in loaded],
        [pltpu.VMEM((256, w), BF) for w in (D0 - EMB, EMB, D0, D0)]
        + [pltpu.VMEM((D0, LAT), BF), pltpu.VMEM((LAT, D0), BF)]
        + [pltpu.VMEM((D0, LAT), F32), pltpu.VMEM((D0, LAT), F32), pltpu.VMEM((1, D0), F32)]
        + [pltpu.VMEM(u_shape, BF)] * 4
        + [pltpu.VMEM(v_shape, BF)] * 2
        + [pltpu.VMEM(bias_rows, F32), pltpu.VMEM(out_shape, BF)]
        + [dma((9,)), dma((6,)), dma((4,))],
        mib=56,
        us=8,
    )
    received = lax.all_to_all(outgoing, TABLE, 0, 0, tiled=True).reshape(SAMP, EMB)
    u_got = shifted([u1, u2, u3], "y")
    v_got = lax.ppermute(v_send, "zl", swap)
    u_shape, v_shape = (160, LAT), (144, LAT)
    v0, v1, v2, v3 = call(
        first_v_kernel,
        [(VMEM, v_shape, F32)] + [(HBM, v_shape, BF)] * 3,
        [place] + near(v_keep, v_got),
        [pltpu.VMEM((544, LAT), F32)] + [pltpu.VMEM(v_shape, BF)] * 3 + [dma((4,))],
        us=2,
    )
    v_got = shifted([v1, v2, v3], "y")
    u_keep, u_send = call(
        first_u_kernel,
        [(VMEM, u_shape, F32), (HBM, u_shape, BF)],
        [place] + near(u0, *u_got) + [(ANY, v0)],
        [pltpu.VMEM((288, LAT), F32), pltpu.VMEM(u_shape, BF), dma((1,))],
        us=100,
    )
    found, pos = call(
        index_kernel,
        [(VMEM, (8, SAMP), F32), (VMEM, (N_REP, 16, 128), BF)],
        near(uniq_rows.reshape(1, UNIQ), lookup_slot.reshape(SAMP, 2).T) + [(ANY, u_keep)],
        mib=24,
    )
    (payload,) = call(
        rows_kernel,
        [(HBM, (N_REP, PAYLOAD, EMB), BF)],
        near(found, received, pos) + [(ANY, u_keep)],
        [pltpu.VMEM((2, 4 * CAP, SAMP), BF), pltpu.VMEM((N_REP, PAYLOAD, EMB), BF), dma((4,))],
        us=7,
    )
    u_got = lax.ppermute(u_send, "zl", swap)
    flat = [(0, 1), (1, 0), (2, 3), (3, 2)]
    cross = [(0, 3), (3, 0), (1, 2), (2, 1)]

    def halve(kernel, ins, in_rows, rows, axis, pairs, us=2, after=()):
        kept, sent = call(
            kernel,
            [(VMEM, (rows, LAT), F32), (HBM, (rows, LAT), BF)],
            [place] + near(*ins) + [(ANY, a) for a in after],
            [pltpu.VMEM((in_rows, LAT), F32), pltpu.VMEM((rows, LAT), BF), dma((1,))],
            us=us,
        )
        return kept, lax.ppermute(sent, axis, pairs)

    both = halve(second_sum_kernel, (u_keep, u_got, v0, *v_got), LAT, 208, "zh", flat, after=(payload,))
    gathered = lax.all_to_all(payload, REP, 0, 0, tiled=True)
    both = halve(third_sum_kernel, both, 208, 112, "x", flat, us=100)
    both = halve(fourth_sum_kernel, both, 112, 64, "x", cross)
    both = halve(fifth_sum_kernel, both, 64, 48, "zh", cross)
    part_u, part_v, whole_bias = call(
        last_kernel,
        [(VMEM, (LATP, FEAT), F32), (VMEM, (LATP, FEAT), F32), (VMEM, (D0 // 128, 128), F32)],
        near(*both),
    )
    (row_part,) = call(keep_kernel, [(VMEM, (KEEP, EMB), F32)], near(gathered))
    return part_u, part_v.T, whole_bias.reshape(D0), row_part.reshape(1, KEEP, EMB)


def solution(mesh):
    fine = Mesh(np.asarray(mesh.devices).reshape(4, 4, 2, 4, 2), ("zh", "x", "zl", "y", "c"))
    every = P(REP + TABLE, None)
    placed = (every, every, every, P(), P(), P(), P(REP, TABLE, None), P(REP, TABLE, None))
    return jax.shard_map(
        shards,
        mesh=fine,
        in_specs=placed,
        out_specs=(P(REP, TABLE), P(TABLE, REP), P(), P(TABLE, REP, None)),
        check_vma=False,
    )
```

```python
import jax
import jax.numpy as jnp
import numpy as np
from jax import lax
from jax.experimental import pallas as pl
from jax.experimental.pallas import tpu as pltpu
from jax.sharding import Mesh, PartitionSpec as P

BF = jnp.bfloat16
F32 = jnp.float32
TABLE = ("zl", "y", "c")
REP = ("zh", "x")
EMB = 128
LAT = 384
N_TAB = 16
N_REP = 16
D0 = 2176
FEAT = 136
LATP = 24
KEEP = 512
CAP = 160
SLOTS = N_REP * CAP
PAYLOAD = CAP + 16
UNIQ = 2048
SAMP = 2048
SCALE = float(32768) ** -0.5

HBM = pl.BlockSpec(memory_space=pltpu.HBM)
ANY = pl.BlockSpec(memory_space=pl.ANY)
VMEM = pl.BlockSpec(memory_space=pltpu.VMEM)
SMEM = pl.BlockSpec(memory_space=pltpu.SMEM)


def params(mib):
    return pltpu.CompilerParams(vmem_limit_bytes=mib * 1024 * 1024)


def coords(place_ref):
    i = place_ref[0]
    return (
        lax.shift_right_logical(i, 6),
        jnp.bitwise_and(lax.shift_right_logical(i, 4), 3),
        jnp.bitwise_and(lax.shift_right_logical(i, 3), 1),
        jnp.bitwise_and(lax.shift_right_logical(i, 1), 3),
        jnp.bitwise_and(i, 1),
    )


def nn(a, b):
    return lax.dot_general(a, b, (((1,), (0,)), ((), ())), preferred_element_type=F32)


def nt(a, b):
    return lax.dot_general(a, b, (((1,), (1,)), ((), ())), preferred_element_type=F32)


def tn(a, b):
    return lax.dot_general(a, b, (((0,), (0,)), ((), ())), preferred_element_type=F32)


def times(a, b):
    return (a.astype(F32) * b.astype(F32)).astype(BF)


def weight_kernel(
    place_ref, pooled_hbm, pooled2_hbm, dense_hbm, dense2_hbm, v_hbm, cot_hbm, cot2_hbm, u_hbm, bias_hbm,
    u0, u1, u2, u3, v_keep, v_send, out_hbm,
    pooled_ref, dense_ref, cot_ref, mix_ref, v_ref, u_ref,
    gu, gv, bias_row, bu0, bu1, bu2, bu3, bk, bs, bias_ref, out_ref, load_sems, sems, out_sems,
):
    own, other = slice(0, 128), slice(128, 256)
    pairs = (
        (pooled_hbm, pooled_ref.at[own, :]), (pooled2_hbm, pooled_ref.at[other, :]),
        (dense_hbm, dense_ref.at[own, :]), (dense2_hbm, dense_ref.at[other, :]),
        (v_hbm, v_ref), (cot_hbm, cot_ref.at[own, :]), (cot2_hbm, cot_ref.at[other, :]), (u_hbm, u_ref),
        (bias_hbm, bias_ref),
    )
    loads = [pltpu.make_async_copy(src, dst, load_sems.at[i]) for i, (src, dst) in enumerate(pairs)]
    for load in loads:
        load.start()
    for load in loads[:5]:
        load.wait()
    lat = (nn(dense_ref[...], v_ref[:EMB, :]) + nn(pooled_ref[...], v_ref[EMB:, :])).astype(BF)
    for load in loads[5:7]:
        load.wait()
    mix_ref[:, :EMB] = times(cot_ref[:, :EMB], dense_ref[...])
    mix_ref[:, EMB:] = times(cot_ref[:, EMB:], pooled_ref[...])
    for load in loads[7:]:
        load.wait()
    gl = nt(mix_ref[...], u_ref[...]).astype(BF)
    bias_row[...] = jnp.sum(mix_ref[...].astype(F32), axis=0, keepdims=True)
    gu[...] = tn(mix_ref[...], lat)
    gv[:EMB, :] = tn(dense_ref[...], gl)
    gv[EMB:, :] = tn(pooled_ref[...], gl)
    high = bias_row[...].astype(BF)
    low = (bias_row[...] - high.astype(F32)).astype(BF)
    tail = jnp.zeros((1, 6 * LAT - D0), BF)
    rows = []
    for part in (high, low):
        whole = jnp.concatenate([part, tail], axis=1)
        rows += [whole[:, k * LAT : (k + 1) * LAT].astype(F32) for k in range(6)]
    rows.append(jnp.zeros((4, LAT), F32))
    bias_block = jnp.concatenate(rows, axis=0).astype(BF)
    _, _, zl, y, c = coords(place_ref)
    copies = []

    def block(g, zl, y):
        start = pl.multiple_of((zl * 8 + y * 2 + c) * FEAT, 8)
        return g[pl.ds(start, FEAT), :]

    def leave(buffer, out):
        copy = pltpu.make_async_copy(buffer, out, sems.at[len(copies)])
        copy.start()
        copies.append(copy)

    for s, (buffer, out) in enumerate(((bu0, u0), (bu1, u1), (bu2, u2), (bu3, u3))):
        dest_y = lax.rem(y + s, 4)
        buffer[0:272, :] = jnp.concatenate([block(gu, 0, dest_y), block(gu, 1, dest_y)], axis=0).astype(BF)
        buffer[272:288, :] = bias_block
        leave(buffer, out)
    for half, buffer, out in ((zl, bk, v_keep), (1 - zl, bs, v_send)):
        for i in range(2):
            pair = jnp.concatenate([block(gv, half, 2 * i), block(gv, half, 2 * i + 1)], axis=0)
            buffer[i * 272 : (i + 1) * 272, :] = pair.astype(BF)
        leave(buffer, out)
    latent, grad_latent = lat[0:128, :], gl[0:128, :]
    for t in range(0, N_TAB, 2):
        cols = slice(EMB + t * EMB, EMB + (t + 2) * EMB)
        bias = jnp.concatenate([bias_ref[t + 1 : t + 2, :], bias_ref[t + 2 : t + 3, :]], axis=1)
        mixing = nn(latent, u_ref[:, cols]) + bias
        backward = nt(grad_latent, v_ref[cols, :])
        grads = (cot_ref[0:128, cols].astype(F32) * (mixing + 1.0) + backward).astype(BF)
        out_ref[t] = grads[:, :EMB]
        out_ref[t + 1] = grads[:, EMB:]
        if t % 4 == 2:
            some = slice(t - 2, t + 2)
            copy = pltpu.make_async_copy(out_ref.at[some], out_hbm.at[some], out_sems.at[t // 4])
            copy.start()
            copies.append(copy)
    for copy in copies:
        copy.wait()


def bias_again(block):
    total = block[0:6, :] + block[6:12, :]
    high = total.astype(BF).astype(F32)
    low = (total - high).astype(BF).astype(F32)
    return jnp.concatenate([high, low, jnp.zeros((4, LAT), F32)], axis=0)


def first_u_kernel(place_ref, m0, m1, m2, m3, _, keep_ref, send_ref, acc, buffer, sem):
    acc[...] = (m0[...].astype(F32) + m1[...].astype(F32)) + (m2[...].astype(F32) + m3[...].astype(F32))
    _, _, zl, _, _ = coords(place_ref)
    rest = [jnp.zeros((8, LAT), F32), bias_again(acc[272:288, :])]
    kept = pick(acc, [zl * FEAT], FEAT) + rest
    split(keep_ref, send_ref, buffer, sem, kept, pick(acc, [(1 - zl) * FEAT], FEAT) + rest)


def first_v_kernel(place_ref, own, got, v0, v1, v2, v3, acc, b1, b2, b3, sems):
    acc[...] = own[...].astype(F32) + got[...].astype(F32)
    _, _, _, y, _ = coords(place_ref)
    gap = [jnp.zeros((8, LAT), F32)]
    copies = []
    for s, buffer, out in ((1, b1, v1), (2, b2, v2), (3, b3, v3)):
        block = pick(acc, [lax.rem(y + s, 4) * FEAT], FEAT)
        buffer[...] = jnp.concatenate(block + gap, axis=0).astype(BF)
        copy = pltpu.make_async_copy(buffer, out, sems.at[s])
        copy.start()
        copies.append(copy)
    v0[...] = jnp.concatenate(pick(acc, [y * FEAT], FEAT) + gap, axis=0)
    for copy in copies:
        copy.wait()


def pick(ref, starts, rows):
    return [ref[pl.ds(pl.multiple_of(start, 8), rows), :] for start in starts]


def split(keep_ref, send_ref, buffer, sem, kept, sent):
    buffer[...] = jnp.concatenate(sent, axis=0).astype(BF)
    copy = pltpu.make_async_copy(buffer, send_ref, sem.at[0])
    copy.start()
    keep_ref[...] = jnp.concatenate(kept, axis=0)
    copy.wait()


def second_sum_kernel(
    place_ref, u_keep, u_got, v0, v1, v2, v3, _, keep_ref, send_ref, flip, buffer, sem
):
    u = u_keep[...] + u_got[...].astype(F32)
    v = (v0[...] + v1[...].astype(F32)) + (v2[...].astype(F32) + v3[...].astype(F32))
    bias = bias_again(u[144:160, :])
    stacked = jnp.concatenate(
        [u[0:128], v[0:128], u[128:136], v[128:136], jnp.zeros((112, LAT), F32)], axis=0
    )
    flip[...] = stacked.T
    zh, x, _, _, _ = coords(place_ref)

    def rows_of(dest):
        order = (x, 3 - x, jnp.bitwise_xor(x, 1), jnp.bitwise_xor(x, 2))
        return pick(flip, [(dest * 4 + dest_x) * LATP for dest_x in order], LATP)

    kept = rows_of(zh) + rows_of(3 - zh) + [bias]
    sent = rows_of(jnp.bitwise_xor(zh, 1)) + rows_of(jnp.bitwise_xor(zh, 2)) + [bias]
    split(keep_ref, send_ref, buffer, sem, kept, sent)


def third_sum_kernel(_, keep, got, keep_ref, send_ref, acc, buffer, sem):
    acc[...] = keep[...] + got[...].astype(F32)
    bias = bias_again(acc[192:208, :])
    kept = [acc[0:48, :], acc[96:144, :], bias]
    split(keep_ref, send_ref, buffer, sem, kept, [acc[48:96, :], acc[144:192, :], bias])


def fourth_sum_kernel(_, keep, got, keep_ref, send_ref, acc, buffer, sem):
    acc[...] = keep[...] + got[...].astype(F32)
    bias = bias_again(acc[96:112, :])
    kept = [acc[0:24, :], acc[48:72, :], bias]
    split(keep_ref, send_ref, buffer, sem, kept, [acc[24:48, :], acc[72:96, :], bias])


def fifth_sum_kernel(_, keep, got, keep_ref, send_ref, acc, buffer, sem):
    acc[...] = keep[...] + got[...].astype(F32)
    bias = bias_again(acc[48:64, :])
    gap = jnp.zeros((8, LAT), F32)
    split(keep_ref, send_ref, buffer, sem, [acc[0:24, :], gap, bias], [acc[24:48, :], gap, bias])


def last_kernel(keep, got, u_ref, v_ref, bias_ref):
    total = keep[...] + got[...].astype(F32)
    total = total * SCALE
    u_ref[:, 0:128] = total[0:LATP, 0:128]
    u_ref[:, 128:136] = total[0:LATP, 256:264]
    v_ref[:, 0:128] = total[0:LATP, 128:256]
    v_ref[:, 128:136] = total[0:LATP, 264:272]
    bias = total[32:38, :] + total[38:44, :]
    for j in range(D0 // 128):
        k, at = j // 3, (j % 3) * 128
        bias_ref[j : j + 1, :] = bias[k : k + 1, at : at + 128]


def index_kernel(uniq_ref, slot_ref, _, found_ref, pos_ref):
    uniq = uniq_ref[...]
    keeper = lax.shift_right_logical(uniq, 9)
    row = jnp.bitwise_and(uniq, KEEP - 1)
    upper = (
        lax.broadcasted_iota(jnp.int32, (128, 128), 0) <= lax.broadcasted_iota(jnp.int32, (128, 128), 1)
    ).astype(F32).astype(BF)
    which = lax.broadcasted_iota(jnp.int32, (N_REP, 128), 0)
    blocks = [keeper[:, b * 128 : (b + 1) * 128] for b in range(UNIQ // 128)]
    members = [(which == own).astype(F32) for own in blocks]
    running = nn(jnp.concatenate(members, axis=0).astype(BF), upper)
    carry = jnp.zeros((N_REP, 1), F32)
    ranks, keepers = [], [own.astype(F32) for own in blocks]
    for b, member in enumerate(members):
        inside = running[b * N_REP : (b + 1) * N_REP, :]
        ranks.append(jnp.sum(member * (inside + (carry - 1.0)), axis=0, keepdims=True))
        carry = carry + inside[:, 127:128]
    member = jnp.concatenate(members, axis=1)
    rank = jnp.concatenate(ranks, axis=1)
    row_high = lax.shift_right_logical(row, 8).astype(F32)
    row_low = jnp.bitwise_and(row, 255).astype(F32)
    digits = jnp.concatenate([member * row_high, member * row_low], axis=0).astype(BF)
    ranked = lax.broadcasted_iota(jnp.int32, (CAP, UNIQ), 0).astype(F32) == rank
    where = nt(digits, ranked.astype(F32).astype(BF))
    wide = jnp.concatenate([where, jnp.zeros((2 * N_REP, 256 - CAP), F32)], axis=1)
    for k in range(N_REP):
        high, low = wide[k : k + 1, :], wide[N_REP + k : N_REP + k + 1, :]
        block = [high[:, 0:128], high[:, 128:256], low[:, 0:128], low[:, 128:256]]
        pos_ref[k] = jnp.concatenate(block + [jnp.zeros((12, 128), F32)], axis=0).astype(BF)
    table = jnp.concatenate(ranks + keepers, axis=0).astype(BF)
    found = []
    for p in range(2):
        slot = slot_ref[p : p + 1, :]
        low = jnp.bitwise_and(slot, 127)
        high = lax.shift_right_logical(slot, 7)
        hot_low = (lax.broadcasted_iota(jnp.int32, (128, SAMP), 0) == low).astype(F32).astype(BF)
        picked = nn(table, hot_low)
        hot_high = (lax.broadcasted_iota(jnp.int32, (16, SAMP), 0) == high).astype(F32)
        found.append(
            (
                jnp.sum(hot_high * picked[0:16, :], axis=0, keepdims=True),
                jnp.sum(hot_high * picked[16:32, :], axis=0, keepdims=True),
            )
        )
    rows = [row for pair in found for row in pair]
    found_ref[...] = jnp.concatenate(rows + [jnp.zeros((4, SAMP), F32)], axis=0)


def rows_kernel(found_ref, got_ref, pos_ref, _, out_hbm, hot, out_ref, sems):
    places = lax.broadcasted_iota(jnp.int32, (CAP, SAMP), 0).astype(F32).astype(BF)
    one, zero = jnp.ones((CAP, SAMP), BF), jnp.zeros((CAP, SAMP), BF)
    stores = []
    for j in range(2):
        for i in range(8):
            k = j * 8 + i
            hits = []
            for p in range(2):
                at, kept = found_ref[2 * p : 2 * p + 1, :], found_ref[2 * p + 1 : 2 * p + 2, :]
                own = jnp.where(kept == float(k), at, -1.0).astype(BF)
                hits.append(jnp.where(places == own, one, zero))
            hot[j % 2, i * CAP : (i + 1) * CAP, :] = hits[0] + hits[1]
        sums = nn(hot[j % 2], got_ref[...]).astype(BF)
        for i in range(8):
            k = j * 8 + i
            out_ref[k, 0:CAP, :] = sums[i * CAP : (i + 1) * CAP, :]
            out_ref[k, CAP:PAYLOAD, :] = pos_ref[k]
        some = slice(j * 8, j * 8 + 8)
        store = pltpu.make_async_copy(out_ref.at[some], out_hbm.at[some], sems.at[j])
        store.start()
        stores.append(store)
    for store in stores:
        store.wait()


def keep_kernel(got_ref, out_ref):
    names = lax.broadcasted_iota(jnp.int32, (256, CAP), 0).astype(F32).astype(BF)
    one, zero = jnp.ones((256, CAP), BF), jnp.zeros((256, CAP), BF)
    accs = [jnp.zeros((256, EMB), F32) for _ in range(2)]
    for g in range(N_REP):
        pos = got_ref[g, CAP:PAYLOAD, :].astype(F32)
        at = [jnp.concatenate([pos[i : i + 1, :], pos[i + 1 : i + 2, 0 : CAP - 128]], axis=1) for i in (0, 2)]
        for half in range(2):
            own = jnp.where(at[0] == float(half), at[1], -1.0).astype(BF)
            hot = jnp.where(names == own, one, zero)
            accs[half] = accs[half] + nn(hot, got_ref[g, 0:CAP, :])
    for half in range(2):
        out_ref[half * 256 : (half + 1) * 256, :] = accs[half]


def call(kernel, outs, ins, scratch=(), mib=24, spare=None, us=2):
    return pl.pallas_call(
        kernel,
        out_shape=tuple(jax.ShapeDtypeStruct(s, d) for _, s, d in outs),
        in_specs=[spec for spec, _ in ins],
        out_specs=tuple(spec for spec, _, _ in outs),
        scratch_shapes=list(scratch),
        input_output_aliases={} if spare is None else {spare[0]: spare[1]},
        compiler_params=params(mib),
        cost_estimate=pl.CostEstimate(flops=us * 10**9, bytes_accessed=us * 10**6, transcendentals=0),
    )(*[a for _, a in ins])


def near(*arrays):
    return [(VMEM, a) for a in arrays]


def shifted(messages, axis):
    got = {
        s: lax.ppermute(messages[s - 1], axis, [(i, (i + s) % 4) for i in range(4)]) for s in (2, 1, 3)
    }
    return [got[s] for s in (1, 2, 3)]


def shards(dense, pooled, cot, proj_v, proj_u, bias, lookup_slot, uniq_rows):
    place = (SMEM, lax.axis_index(REP + TABLE).astype(jnp.int32).reshape(1))
    swap = [(0, 1), (1, 0)]
    other = [lax.ppermute(a, "c", swap) for a in (dense, pooled, cot)]
    dma = pltpu.SemaphoreType.DMA
    dense2, pooled2, cot2 = other
    u_shape, v_shape = (288, LAT), (544, LAT)
    bias_rows, out_shape = (D0 // 128, 128), (N_TAB, 128, EMB)
    loaded = (pooled, pooled2, dense, dense2, proj_v, cot, cot2, proj_u, bias.reshape(bias_rows))
    u0, u1, u2, u3, v_keep, v_send, outgoing = call(
        weight_kernel,
        [(HBM, u_shape, BF)] * 4 + [(HBM, v_shape, BF)] * 2 + [(HBM, out_shape, BF)],
        [place] + [(HBM, a) for a in loaded],
        [pltpu.VMEM((256, w), BF) for w in (D0 - EMB, EMB, D0, D0)]
        + [pltpu.VMEM((D0, LAT), BF), pltpu.VMEM((LAT, D0), BF)]
        + [pltpu.VMEM((D0, LAT), F32), pltpu.VMEM((D0, LAT), F32), pltpu.VMEM((1, D0), F32)]
        + [pltpu.VMEM(u_shape, BF)] * 4
        + [pltpu.VMEM(v_shape, BF)] * 2
        + [pltpu.VMEM(bias_rows, F32), pltpu.VMEM(out_shape, BF)]
        + [dma((9,)), dma((6,)), dma((4,))],
        mib=56,
        us=8,
    )
    received = lax.all_to_all(outgoing, TABLE, 0, 0, tiled=True).reshape(SAMP, EMB)
    u_got = shifted([u1, u2, u3], "y")
    v_got = lax.ppermute(v_send, "zl", swap)
    u_shape, v_shape = (160, LAT), (144, LAT)
    v0, v1, v2, v3 = call(
        first_v_kernel,
        [(VMEM, v_shape, F32)] + [(HBM, v_shape, BF)] * 3,
        [place] + near(v_keep, v_got),
        [pltpu.VMEM((544, LAT), F32)] + [pltpu.VMEM(v_shape, BF)] * 3 + [dma((4,))],
        us=2,
    )
    v_got = shifted([v1, v2, v3], "y")
    u_keep, u_send = call(
        first_u_kernel,
        [(VMEM, u_shape, F32), (HBM, u_shape, BF)],
        [place] + near(u0, *u_got) + [(ANY, v0)],
        [pltpu.VMEM((288, LAT), F32), pltpu.VMEM(u_shape, BF), dma((1,))],
        us=100,
    )
    found, pos = call(
        index_kernel,
        [(VMEM, (8, SAMP), F32), (VMEM, (N_REP, 16, 128), BF)],
        near(uniq_rows.reshape(1, UNIQ), lookup_slot.reshape(SAMP, 2).T) + [(ANY, u_keep)],
        mib=24,
    )
    (payload,) = call(
        rows_kernel,
        [(HBM, (N_REP, PAYLOAD, EMB), BF)],
        near(found, received, pos) + [(ANY, u_keep)],
        [pltpu.VMEM((2, 8 * CAP, SAMP), BF), pltpu.VMEM((N_REP, PAYLOAD, EMB), BF), dma((2,))],
        us=7,
    )
    u_got = lax.ppermute(u_send, "zl", swap)
    flat = [(0, 1), (1, 0), (2, 3), (3, 2)]
    cross = [(0, 3), (3, 0), (1, 2), (2, 1)]

    def halve(kernel, ins, in_rows, rows, axis, pairs, us=2, after=()):
        kept, sent = call(
            kernel,
            [(VMEM, (rows, LAT), F32), (HBM, (rows, LAT), BF)],
            [place] + near(*ins) + [(ANY, a) for a in after],
            [pltpu.VMEM((in_rows, LAT), F32), pltpu.VMEM((rows, LAT), BF), dma((1,))],
            us=us,
        )
        return kept, lax.ppermute(sent, axis, pairs)

    both = halve(second_sum_kernel, (u_keep, u_got, v0, *v_got), LAT, 208, "zh", flat, after=(payload,))
    gathered = lax.all_to_all(payload, REP, 0, 0, tiled=True)
    both = halve(third_sum_kernel, both, 208, 112, "x", flat, us=100)
    both = halve(fourth_sum_kernel, both, 112, 64, "x", cross)
    both = halve(fifth_sum_kernel, both, 64, 48, "zh", cross)
    part_u, part_v, whole_bias = call(
        last_kernel,
        [(VMEM, (LATP, FEAT), F32), (VMEM, (LATP, FEAT), F32), (VMEM, (D0 // 128, 128), F32)],
        near(*both),
    )
    (row_part,) = call(keep_kernel, [(VMEM, (KEEP, EMB), F32)], near(gathered))
    return part_u, part_v.T, whole_bias.reshape(D0), row_part.reshape(1, KEEP, EMB)


def solution(mesh):
    fine = Mesh(np.asarray(mesh.devices).reshape(4, 4, 2, 4, 2), ("zh", "x", "zl", "y", "c"))
    every = P(REP + TABLE, None)
    placed = (every, every, every, P(), P(), P(), P(REP, TABLE, None), P(REP, TABLE, None))
    return jax.shard_map(
        shards,
        mesh=fine,
        in_specs=placed,
        out_specs=(P(REP, TABLE), P(TABLE, REP), P(), P(TABLE, REP, None)),
        check_vma=False,
    )
```

```python
import jax
import jax.numpy as jnp
import numpy as np
from jax import lax
from jax.experimental import pallas as pl
from jax.experimental.pallas import tpu as pltpu
from jax.sharding import Mesh, PartitionSpec as P

BF = jnp.bfloat16
F32 = jnp.float32
TABLE = ("zl", "y", "c")
REP = ("zh", "x")
EMB = 128
LAT = 384
N_TAB = 16
N_REP = 16
D0 = 2176
FEAT = 136
LATP = 24
KEEP = 512
CAP = 160
SLOTS = N_REP * CAP
PAYLOAD = CAP + 16
UNIQ = 2048
SAMP = 2048
SCALE = float(32768) ** -0.5

HBM = pl.BlockSpec(memory_space=pltpu.HBM)
ANY = pl.BlockSpec(memory_space=pl.ANY)
VMEM = pl.BlockSpec(memory_space=pltpu.VMEM)
SMEM = pl.BlockSpec(memory_space=pltpu.SMEM)


def params(mib):
    return pltpu.CompilerParams(vmem_limit_bytes=mib * 1024 * 1024)


def coords(place_ref):
    i = place_ref[0]
    return (
        lax.shift_right_logical(i, 6),
        jnp.bitwise_and(lax.shift_right_logical(i, 4), 3),
        jnp.bitwise_and(lax.shift_right_logical(i, 3), 1),
        jnp.bitwise_and(lax.shift_right_logical(i, 1), 3),
        jnp.bitwise_and(i, 1),
    )


def nn(a, b):
    return lax.dot_general(a, b, (((1,), (0,)), ((), ())), preferred_element_type=F32)


def nt(a, b):
    return lax.dot_general(a, b, (((1,), (1,)), ((), ())), preferred_element_type=F32)


def tn(a, b):
    return lax.dot_general(a, b, (((0,), (0,)), ((), ())), preferred_element_type=F32)


def times(a, b):
    return (a.astype(F32) * b.astype(F32)).astype(BF)


def weight_kernel(
    place_ref, pooled_hbm, pooled2_hbm, dense_hbm, dense2_hbm, v_hbm, cot_hbm, cot2_hbm, u_hbm, bias_hbm,
    u0, u1, u2, u3, v_keep, v_send, out_hbm,
    pooled_ref, dense_ref, cot_ref, mix_ref, v_ref, u_ref,
    gu, gv, bias_row, bu0, bu1, bu2, bu3, bk, bs, bias_ref, out_ref, load_sems, sems, out_sems,
):
    own, other = slice(0, 128), slice(128, 256)
    pairs = (
        (pooled_hbm, pooled_ref.at[own, :]), (pooled2_hbm, pooled_ref.at[other, :]),
        (dense_hbm, dense_ref.at[own, :]), (dense2_hbm, dense_ref.at[other, :]),
        (v_hbm, v_ref), (cot_hbm, cot_ref.at[own, :]), (cot2_hbm, cot_ref.at[other, :]), (u_hbm, u_ref),
        (bias_hbm, bias_ref),
    )
    loads = [pltpu.make_async_copy(src, dst, load_sems.at[i]) for i, (src, dst) in enumerate(pairs)]
    for load in loads:
        load.start()
    for load in loads[:5]:
        load.wait()
    lat = (nn(dense_ref[...], v_ref[:EMB, :]) + nn(pooled_ref[...], v_ref[EMB:, :])).astype(BF)
    for load in loads[5:7]:
        load.wait()
    mix_ref[:, :EMB] = times(cot_ref[:, :EMB], dense_ref[...])
    mix_ref[:, EMB:] = times(cot_ref[:, EMB:], pooled_ref[...])
    for load in loads[7:]:
        load.wait()
    gl = nt(mix_ref[...], u_ref[...]).astype(BF)
    bias_row[...] = jnp.sum(mix_ref[...].astype(F32), axis=0, keepdims=True)
    gu[...] = tn(mix_ref[...], lat)
    gv[:EMB, :] = tn(dense_ref[...], gl)
    gv[EMB:, :] = tn(pooled_ref[...], gl)
    high = bias_row[...].astype(BF)
    low = (bias_row[...] - high.astype(F32)).astype(BF)
    tail = jnp.zeros((1, 6 * LAT - D0), BF)
    rows = []
    for part in (high, low):
        whole = jnp.concatenate([part, tail], axis=1)
        rows += [whole[:, k * LAT : (k + 1) * LAT].astype(F32) for k in range(6)]
    rows.append(jnp.zeros((4, LAT), F32))
    bias_block = jnp.concatenate(rows, axis=0).astype(BF)
    _, _, zl, y, c = coords(place_ref)
    copies = []

    def block(g, zl, y):
        start = pl.multiple_of((zl * 8 + y * 2 + c) * FEAT, 8)
        return g[pl.ds(start, FEAT), :]

    def leave(buffer, out):
        copy = pltpu.make_async_copy(buffer, out, sems.at[len(copies)])
        copy.start()
        copies.append(copy)

    for s, (buffer, out) in enumerate(((bu0, u0), (bu1, u1), (bu2, u2), (bu3, u3))):
        dest_y = lax.rem(y + s, 4)
        buffer[0:272, :] = jnp.concatenate([block(gu, 0, dest_y), block(gu, 1, dest_y)], axis=0).astype(BF)
        buffer[272:288, :] = bias_block
        leave(buffer, out)
    for half, buffer, out in ((zl, bk, v_keep), (1 - zl, bs, v_send)):
        for i in range(2):
            pair = jnp.concatenate([block(gv, half, 2 * i), block(gv, half, 2 * i + 1)], axis=0)
            buffer[i * 272 : (i + 1) * 272, :] = pair.astype(BF)
        leave(buffer, out)
    latent, grad_latent = lat[0:128, :], gl[0:128, :]
    for t in range(0, N_TAB, 2):
        cols = slice(EMB + t * EMB, EMB + (t + 2) * EMB)
        bias = jnp.concatenate([bias_ref[t + 1 : t + 2, :], bias_ref[t + 2 : t + 3, :]], axis=1)
        mixing = nn(latent, u_ref[:, cols]) + bias
        backward = nt(grad_latent, v_ref[cols, :])
        grads = (cot_ref[0:128, cols].astype(F32) * (mixing + 1.0) + backward).astype(BF)
        out_ref[t] = grads[:, :EMB]
        out_ref[t + 1] = grads[:, EMB:]
        if t % 4 == 2:
            some = slice(t - 2, t + 2)
            copy = pltpu.make_async_copy(out_ref.at[some], out_hbm.at[some], out_sems.at[t // 4])
            copy.start()
            copies.append(copy)
    for copy in copies:
        copy.wait()


def bias_again(block):
    total = block[0:6, :] + block[6:12, :]
    high = total.astype(BF).astype(F32)
    low = (total - high).astype(BF).astype(F32)
    return jnp.concatenate([high, low, jnp.zeros((4, LAT), F32)], axis=0)


def first_u_kernel(place_ref, m0, m1, m2, m3, _, keep_ref, send_ref, acc, buffer, sem):
    acc[...] = (m0[...].astype(F32) + m1[...].astype(F32)) + (m2[...].astype(F32) + m3[...].astype(F32))
    _, _, zl, _, _ = coords(place_ref)
    rest = [jnp.zeros((8, LAT), F32), bias_again(acc[272:288, :])]
    kept = pick(acc, [zl * FEAT], FEAT) + rest
    split(keep_ref, send_ref, buffer, sem, kept, pick(acc, [(1 - zl) * FEAT], FEAT) + rest)


def first_v_kernel(place_ref, own, got, v0, v1, v2, v3, acc, b1, b2, b3, sems):
    acc[...] = own[...].astype(F32) + got[...].astype(F32)
    _, _, _, y, _ = coords(place_ref)
    gap = [jnp.zeros((8, LAT), F32)]
    copies = []
    for s, buffer, out in ((1, b1, v1), (2, b2, v2), (3, b3, v3)):
        block = pick(acc, [lax.rem(y + s, 4) * FEAT], FEAT)
        buffer[...] = jnp.concatenate(block + gap, axis=0).astype(BF)
        copy = pltpu.make_async_copy(buffer, out, sems.at[s])
        copy.start()
        copies.append(copy)
    v0[...] = jnp.concatenate(pick(acc, [y * FEAT], FEAT) + gap, axis=0)
    for copy in copies:
        copy.wait()


def pick(ref, starts, rows):
    return [ref[pl.ds(pl.multiple_of(start, 8), rows), :] for start in starts]


def split(keep_ref, send_ref, buffer, sem, kept, sent):
    buffer[...] = jnp.concatenate(sent, axis=0).astype(BF)
    copy = pltpu.make_async_copy(buffer, send_ref, sem.at[0])
    copy.start()
    keep_ref[...] = jnp.concatenate(kept, axis=0)
    copy.wait()


def second_sum_kernel(
    place_ref, u_keep, u_got, v0, v1, v2, v3, _, keep_ref, send_ref, flip, buffer, sem
):
    u = u_keep[...] + u_got[...].astype(F32)
    v = (v0[...] + v1[...].astype(F32)) + (v2[...].astype(F32) + v3[...].astype(F32))
    bias = bias_again(u[144:160, :])
    stacked = jnp.concatenate(
        [u[0:128], v[0:128], u[128:136], v[128:136], jnp.zeros((112, LAT), F32)], axis=0
    )
    flip[...] = stacked.T
    zh, x, _, _, _ = coords(place_ref)

    def rows_of(dest):
        order = (x, 3 - x, jnp.bitwise_xor(x, 1), jnp.bitwise_xor(x, 2))
        return pick(flip, [(dest * 4 + dest_x) * LATP for dest_x in order], LATP)

    kept = rows_of(zh) + rows_of(3 - zh) + [bias]
    sent = rows_of(jnp.bitwise_xor(zh, 1)) + rows_of(jnp.bitwise_xor(zh, 2)) + [bias]
    split(keep_ref, send_ref, buffer, sem, kept, sent)


def third_sum_kernel(_, keep, got, keep_ref, send_ref, acc, buffer, sem):
    acc[...] = keep[...] + got[...].astype(F32)
    bias = bias_again(acc[192:208, :])
    kept = [acc[0:48, :], acc[96:144, :], bias]
    split(keep_ref, send_ref, buffer, sem, kept, [acc[48:96, :], acc[144:192, :], bias])


def fourth_sum_kernel(_, keep, got, keep_ref, send_ref, acc, buffer, sem):
    acc[...] = keep[...] + got[...].astype(F32)
    bias = bias_again(acc[96:112, :])
    kept = [acc[0:24, :], acc[48:72, :], bias]
    split(keep_ref, send_ref, buffer, sem, kept, [acc[24:48, :], acc[72:96, :], bias])


def fifth_sum_kernel(_, keep, got, keep_ref, send_ref, acc, buffer, sem):
    acc[...] = keep[...] + got[...].astype(F32)
    bias = bias_again(acc[48:64, :])
    gap = jnp.zeros((8, LAT), F32)
    split(keep_ref, send_ref, buffer, sem, [acc[0:24, :], gap, bias], [acc[24:48, :], gap, bias])


def last_kernel(keep, got, u_ref, v_ref, bias_ref):
    total = keep[...] + got[...].astype(F32)
    total = total * SCALE
    u_ref[:, 0:128] = total[0:LATP, 0:128]
    u_ref[:, 128:136] = total[0:LATP, 256:264]
    v_ref[:, 0:128] = total[0:LATP, 128:256]
    v_ref[:, 128:136] = total[0:LATP, 264:272]
    bias = total[32:38, :] + total[38:44, :]
    for j in range(D0 // 128):
        k, at = j // 3, (j % 3) * 128
        bias_ref[j : j + 1, :] = bias[k : k + 1, at : at + 128]


def index_kernel(uniq_ref, slot_ref, _, found_ref, pos_ref):
    uniq = uniq_ref[...]
    keeper = lax.shift_right_logical(uniq, 9)
    row = jnp.bitwise_and(uniq, KEEP - 1)
    upper = (
        lax.broadcasted_iota(jnp.int32, (128, 128), 0) <= lax.broadcasted_iota(jnp.int32, (128, 128), 1)
    ).astype(F32).astype(BF)
    which = lax.broadcasted_iota(jnp.int32, (N_REP, 128), 0)
    blocks = [keeper[:, b * 128 : (b + 1) * 128] for b in range(UNIQ // 128)]
    members = [(which == own).astype(F32) for own in blocks]
    running = nn(jnp.concatenate(members, axis=0).astype(BF), upper)
    carry = jnp.zeros((N_REP, 1), F32)
    ranks, keepers = [], [own.astype(F32) for own in blocks]
    for b, member in enumerate(members):
        inside = running[b * N_REP : (b + 1) * N_REP, :]
        ranks.append(jnp.sum(member * (inside + (carry - 1.0)), axis=0, keepdims=True))
        carry = carry + inside[:, 127:128]
    member = jnp.concatenate(members, axis=1)
    rank = jnp.concatenate(ranks, axis=1)
    row_high = lax.shift_right_logical(row, 8).astype(F32)
    row_low = jnp.bitwise_and(row, 255).astype(F32)
    digits = jnp.concatenate([member * row_high, member * row_low], axis=0).astype(BF)
    ranked = lax.broadcasted_iota(jnp.int32, (CAP, UNIQ), 0).astype(F32) == rank
    where = nt(digits, ranked.astype(F32).astype(BF))
    wide = jnp.concatenate([where, jnp.zeros((2 * N_REP, 256 - CAP), F32)], axis=1)
    for k in range(N_REP):
        high, low = wide[k : k + 1, :], wide[N_REP + k : N_REP + k + 1, :]
        block = [high[:, 0:128], high[:, 128:256], low[:, 0:128], low[:, 128:256]]
        pos_ref[k] = jnp.concatenate(block + [jnp.zeros((12, 128), F32)], axis=0).astype(BF)
    table = jnp.concatenate(ranks + keepers, axis=0).astype(BF)
    found = []
    for p in range(2):
        slot = slot_ref[p : p + 1, :]
        low = jnp.bitwise_and(slot, 127)
        high = lax.shift_right_logical(slot, 7)
        hot_low = (lax.broadcasted_iota(jnp.int32, (128, SAMP), 0) == low).astype(F32).astype(BF)
        picked = nn(table, hot_low)
        hot_high = (lax.broadcasted_iota(jnp.int32, (16, SAMP), 0) == high).astype(F32)
        found.append(
            (
                jnp.sum(hot_high * picked[0:16, :], axis=0, keepdims=True),
                jnp.sum(hot_high * picked[16:32, :], axis=0, keepdims=True),
            )
        )
    rows = [row for pair in found for row in pair]
    found_ref[...] = jnp.concatenate(rows + [jnp.zeros((4, SAMP), F32)], axis=0)


def rows_kernel(found_ref, got_ref, pos_ref, _, out_hbm, hot, out_ref, sems):
    places = lax.broadcasted_iota(jnp.int32, (CAP, SAMP), 0).astype(F32).astype(BF)
    one, zero = jnp.ones((CAP, SAMP), BF), jnp.zeros((CAP, SAMP), BF)
    stores = []
    for j in range(2):
        for i in range(8):
            k = j * 8 + i
            hits = []
            for p in range(2):
                at, kept = found_ref[2 * p : 2 * p + 1, :], found_ref[2 * p + 1 : 2 * p + 2, :]
                own = jnp.where(kept == float(k), at, -1.0).astype(BF)
                hits.append(jnp.where(places == own, one, zero))
            hot[j % 2, i * CAP : (i + 1) * CAP, :] = hits[0] + hits[1]
        sums = nn(hot[j % 2], got_ref[...]).astype(BF)
        for i in range(8):
            k = j * 8 + i
            out_ref[k, 0:CAP, :] = sums[i * CAP : (i + 1) * CAP, :]
            out_ref[k, CAP:PAYLOAD, :] = pos_ref[k]
        some = slice(j * 8, j * 8 + 8)
        store = pltpu.make_async_copy(out_ref.at[some], out_hbm.at[some], sems.at[j])
        store.start()
        stores.append(store)
    for store in stores:
        store.wait()


def keep_kernel(got_ref, out_ref):
    wide = N_REP * PAYLOAD
    nowhere = jnp.full((1, PAYLOAD - CAP), -1.0, F32)
    digits = []
    for i in (0, 2):
        pieces = []
        for g in range(N_REP):
            pos = got_ref[g, CAP:PAYLOAD, :].astype(F32)
            pieces += [pos[i : i + 1, :], pos[i + 1 : i + 2, 0 : CAP - 128], nowhere]
        digits.append(jnp.concatenate(pieces, axis=1))
    got = got_ref[...].reshape(wide, EMB)
    names = lax.broadcasted_iota(jnp.int32, (256, wide), 0).astype(F32).astype(BF)
    one, zero = jnp.ones((256, wide), BF), jnp.zeros((256, wide), BF)
    for half in range(2):
        own = jnp.where(digits[0] == float(half), digits[1], -1.0).astype(BF)
        out_ref[half * 256 : (half + 1) * 256, :] = nn(jnp.where(names == own, one, zero), got)


def call(kernel, outs, ins, scratch=(), mib=24, spare=None, us=2):
    return pl.pallas_call(
        kernel,
        out_shape=tuple(jax.ShapeDtypeStruct(s, d) for _, s, d in outs),
        in_specs=[spec for spec, _ in ins],
        out_specs=tuple(spec for spec, _, _ in outs),
        scratch_shapes=list(scratch),
        input_output_aliases={} if spare is None else {spare[0]: spare[1]},
        compiler_params=params(mib),
        cost_estimate=pl.CostEstimate(flops=us * 10**9, bytes_accessed=us * 10**6, transcendentals=0),
    )(*[a for _, a in ins])


def near(*arrays):
    return [(VMEM, a) for a in arrays]


def shifted(messages, axis):
    got = {
        s: lax.ppermute(messages[s - 1], axis, [(i, (i + s) % 4) for i in range(4)]) for s in (2, 1, 3)
    }
    return [got[s] for s in (1, 2, 3)]


def shards(dense, pooled, cot, proj_v, proj_u, bias, lookup_slot, uniq_rows):
    place = (SMEM, lax.axis_index(REP + TABLE).astype(jnp.int32).reshape(1))
    swap = [(0, 1), (1, 0)]
    other = [lax.ppermute(a, "c", swap) for a in (dense, pooled, cot)]
    dma = pltpu.SemaphoreType.DMA
    dense2, pooled2, cot2 = other
    u_shape, v_shape = (288, LAT), (544, LAT)
    bias_rows, out_shape = (D0 // 128, 128), (N_TAB, 128, EMB)
    loaded = (pooled, pooled2, dense, dense2, proj_v, cot, cot2, proj_u, bias.reshape(bias_rows))
    u0, u1, u2, u3, v_keep, v_send, outgoing = call(
        weight_kernel,
        [(HBM, u_shape, BF)] * 4 + [(HBM, v_shape, BF)] * 2 + [(HBM, out_shape, BF)],
        [place] + [(HBM, a) for a in loaded],
        [pltpu.VMEM((256, w), BF) for w in (D0 - EMB, EMB, D0, D0)]
        + [pltpu.VMEM((D0, LAT), BF), pltpu.VMEM((LAT, D0), BF)]
        + [pltpu.VMEM((D0, LAT), F32), pltpu.VMEM((D0, LAT), F32), pltpu.VMEM((1, D0), F32)]
        + [pltpu.VMEM(u_shape, BF)] * 4
        + [pltpu.VMEM(v_shape, BF)] * 2
        + [pltpu.VMEM(bias_rows, F32), pltpu.VMEM(out_shape, BF)]
        + [dma((9,)), dma((6,)), dma((4,))],
        mib=56,
        us=8,
    )
    received = lax.all_to_all(outgoing, TABLE, 0, 0, tiled=True).reshape(SAMP, EMB)
    u_got = shifted([u1, u2, u3], "y")
    v_got = lax.ppermute(v_send, "zl", swap)
    u_shape, v_shape = (160, LAT), (144, LAT)
    v0, v1, v2, v3 = call(
        first_v_kernel,
        [(VMEM, v_shape, F32)] + [(HBM, v_shape, BF)] * 3,
        [place] + near(v_keep, v_got),
        [pltpu.VMEM((544, LAT), F32)] + [pltpu.VMEM(v_shape, BF)] * 3 + [dma((4,))],
        us=2,
    )
    v_got = shifted([v1, v2, v3], "y")
    u_keep, u_send = call(
        first_u_kernel,
        [(VMEM, u_shape, F32), (HBM, u_shape, BF)],
        [place] + near(u0, *u_got) + [(ANY, v0)],
        [pltpu.VMEM((288, LAT), F32), pltpu.VMEM(u_shape, BF), dma((1,))],
        us=100,
    )
    found, pos = call(
        index_kernel,
        [(VMEM, (8, SAMP), F32), (VMEM, (N_REP, 16, 128), BF)],
        near(uniq_rows.reshape(1, UNIQ), lookup_slot.reshape(SAMP, 2).T) + [(ANY, u_keep)],
        mib=24,
    )
    (payload,) = call(
        rows_kernel,
        [(HBM, (N_REP, PAYLOAD, EMB), BF)],
        near(found, received, pos) + [(ANY, u_keep)],
        [pltpu.VMEM((2, 8 * CAP, SAMP), BF), pltpu.VMEM((N_REP, PAYLOAD, EMB), BF), dma((2,))],
        us=7,
    )
    u_got = lax.ppermute(u_send, "zl", swap)
    flat = [(0, 1), (1, 0), (2, 3), (3, 2)]
    cross = [(0, 3), (3, 0), (1, 2), (2, 1)]

    def halve(kernel, ins, in_rows, rows, axis, pairs, us=2, after=()):
        kept, sent = call(
            kernel,
            [(VMEM, (rows, LAT), F32), (HBM, (rows, LAT), BF)],
            [place] + near(*ins) + [(ANY, a) for a in after],
            [pltpu.VMEM((in_rows, LAT), F32), pltpu.VMEM((rows, LAT), BF), dma((1,))],
            us=us,
        )
        return kept, lax.ppermute(sent, axis, pairs)

    both = halve(second_sum_kernel, (u_keep, u_got, v0, *v_got), LAT, 208, "zh", flat, after=(payload,))
    gathered = lax.all_to_all(payload, REP, 0, 0, tiled=True)
    both = halve(third_sum_kernel, both, 208, 112, "x", flat, us=100)
    both = halve(fourth_sum_kernel, both, 112, 64, "x", cross)
    both = halve(fifth_sum_kernel, both, 64, 48, "zh", cross)
    part_u, part_v, whole_bias = call(
        last_kernel,
        [(VMEM, (LATP, FEAT), F32), (VMEM, (LATP, FEAT), F32), (VMEM, (D0 // 128, 128), F32)],
        near(*both),
    )
    (row_part,) = call(keep_kernel, [(VMEM, (KEEP, EMB), F32)], near(gathered))
    return part_u, part_v.T, whole_bias.reshape(D0), row_part.reshape(1, KEEP, EMB)


def solution(mesh):
    fine = Mesh(np.asarray(mesh.devices).reshape(4, 4, 2, 4, 2), ("zh", "x", "zl", "y", "c"))
    every = P(REP + TABLE, None)
    placed = (every, every, every, P(), P(), P(), P(REP, TABLE, None), P(REP, TABLE, None))
    return jax.shard_map(
        shards,
        mesh=fine,
        in_specs=placed,
        out_specs=(P(REP, TABLE), P(TABLE, REP), P(), P(TABLE, REP, None)),
        check_vma=False,
    )
```

```python
import jax
import jax.numpy as jnp
import numpy as np
from jax import lax
from jax.experimental import pallas as pl
from jax.experimental.pallas import tpu as pltpu
from jax.sharding import Mesh, PartitionSpec as P

BF = jnp.bfloat16
F32 = jnp.float32
TABLE = ("zl", "y", "c")
REP = ("zh", "x")
EMB = 128
LAT = 384
N_TAB = 16
N_REP = 16
D0 = 2176
FEAT = 136
LATP = 24
KEEP = 512
CAP = 160
SLOTS = N_REP * CAP
PAYLOAD = CAP + 8
UNIQ = 2048
SAMP = 2048
SCALE = float(32768) ** -0.5

HBM = pl.BlockSpec(memory_space=pltpu.HBM)
ANY = pl.BlockSpec(memory_space=pl.ANY)
VMEM = pl.BlockSpec(memory_space=pltpu.VMEM)
SMEM = pl.BlockSpec(memory_space=pltpu.SMEM)


def params(mib):
    return pltpu.CompilerParams(vmem_limit_bytes=mib * 1024 * 1024)


def coords(place_ref):
    i = place_ref[0]
    return (
        lax.shift_right_logical(i, 6),
        jnp.bitwise_and(lax.shift_right_logical(i, 4), 3),
        jnp.bitwise_and(lax.shift_right_logical(i, 3), 1),
        jnp.bitwise_and(lax.shift_right_logical(i, 1), 3),
        jnp.bitwise_and(i, 1),
    )


def nn(a, b):
    return lax.dot_general(a, b, (((1,), (0,)), ((), ())), preferred_element_type=F32)


def nt(a, b):
    return lax.dot_general(a, b, (((1,), (1,)), ((), ())), preferred_element_type=F32)


def tn(a, b):
    return lax.dot_general(a, b, (((0,), (0,)), ((), ())), preferred_element_type=F32)


def times(a, b):
    return (a.astype(F32) * b.astype(F32)).astype(BF)


def weight_kernel(
    place_ref, pooled_hbm, pooled2_hbm, dense_hbm, dense2_hbm, v_hbm, cot_hbm, cot2_hbm, u_hbm, bias_hbm,
    u0, u1, u2, u3, v_keep, v_send, out_hbm,
    pooled_ref, dense_ref, cot_ref, mix_ref, v_ref, u_ref,
    gu, gv, bias_row, bu0, bu1, bu2, bu3, bk, bs, bias_ref, out_ref, load_sems, sems, out_sems,
):
    own, other = slice(0, 128), slice(128, 256)
    pairs = (
        (pooled_hbm, pooled_ref.at[own, :]), (pooled2_hbm, pooled_ref.at[other, :]),
        (dense_hbm, dense_ref.at[own, :]), (dense2_hbm, dense_ref.at[other, :]),
        (v_hbm, v_ref), (cot_hbm, cot_ref.at[own, :]), (cot2_hbm, cot_ref.at[other, :]), (u_hbm, u_ref),
        (bias_hbm, bias_ref),
    )
    loads = [pltpu.make_async_copy(src, dst, load_sems.at[i]) for i, (src, dst) in enumerate(pairs)]
    for load in loads:
        load.start()
    for load in loads[:5]:
        load.wait()
    lat = (nn(dense_ref[...], v_ref[:EMB, :]) + nn(pooled_ref[...], v_ref[EMB:, :])).astype(BF)
    for load in loads[5:7]:
        load.wait()
    mix_ref[:, :EMB] = times(cot_ref[:, :EMB], dense_ref[...])
    mix_ref[:, EMB:] = times(cot_ref[:, EMB:], pooled_ref[...])
    for load in loads[7:]:
        load.wait()
    gl = nt(mix_ref[...], u_ref[...]).astype(BF)
    bias_row[...] = jnp.sum(mix_ref[...].astype(F32), axis=0, keepdims=True)
    gu[...] = tn(mix_ref[...], lat)
    gv[:EMB, :] = tn(dense_ref[...], gl)
    gv[EMB:, :] = tn(pooled_ref[...], gl)
    high = bias_row[...].astype(BF)
    low = (bias_row[...] - high.astype(F32)).astype(BF)
    tail = jnp.zeros((1, 6 * LAT - D0), BF)
    rows = []
    for part in (high, low):
        whole = jnp.concatenate([part, tail], axis=1)
        rows += [whole[:, k * LAT : (k + 1) * LAT].astype(F32) for k in range(6)]
    rows.append(jnp.zeros((4, LAT), F32))
    bias_block = jnp.concatenate(rows, axis=0).astype(BF)
    _, _, zl, y, c = coords(place_ref)
    copies = []

    def block(g, zl, y):
        start = pl.multiple_of((zl * 8 + y * 2 + c) * FEAT, 8)
        return g[pl.ds(start, FEAT), :]

    def leave(buffer, out):
        copy = pltpu.make_async_copy(buffer, out, sems.at[len(copies)])
        copy.start()
        copies.append(copy)

    for s, (buffer, out) in enumerate(((bu0, u0), (bu1, u1), (bu2, u2), (bu3, u3))):
        dest_y = lax.rem(y + s, 4)
        buffer[0:272, :] = jnp.concatenate([block(gu, 0, dest_y), block(gu, 1, dest_y)], axis=0).astype(BF)
        buffer[272:288, :] = bias_block
        leave(buffer, out)
    for half, buffer, out in ((zl, bk, v_keep), (1 - zl, bs, v_send)):
        for i in range(2):
            pair = jnp.concatenate([block(gv, half, 2 * i), block(gv, half, 2 * i + 1)], axis=0)
            buffer[i * 272 : (i + 1) * 272, :] = pair.astype(BF)
        leave(buffer, out)
    latent, grad_latent = lat[0:128, :], gl[0:128, :]
    for t in range(0, N_TAB, 2):
        cols = slice(EMB + t * EMB, EMB + (t + 2) * EMB)
        bias = jnp.concatenate([bias_ref[t + 1 : t + 2, :], bias_ref[t + 2 : t + 3, :]], axis=1)
        mixing = nn(latent, u_ref[:, cols]) + bias
        backward = nt(grad_latent, v_ref[cols, :])
        grads = (cot_ref[0:128, cols].astype(F32) * (mixing + 1.0) + backward).astype(BF)
        out_ref[t] = grads[:, :EMB]
        out_ref[t + 1] = grads[:, EMB:]
        if t % 4 == 2:
            some = slice(t - 2, t + 2)
            copy = pltpu.make_async_copy(out_ref.at[some], out_hbm.at[some], out_sems.at[t // 4])
            copy.start()
            copies.append(copy)
    for copy in copies:
        copy.wait()


def bias_again(block):
    total = block[0:6, :] + block[6:12, :]
    high = total.astype(BF).astype(F32)
    low = (total - high).astype(BF).astype(F32)
    return jnp.concatenate([high, low, jnp.zeros((4, LAT), F32)], axis=0)


def first_u_kernel(place_ref, m0, m1, m2, m3, _, keep_ref, send_ref, acc, buffer, sem):
    acc[...] = (m0[...].astype(F32) + m1[...].astype(F32)) + (m2[...].astype(F32) + m3[...].astype(F32))
    _, _, zl, _, _ = coords(place_ref)
    rest = [jnp.zeros((8, LAT), F32), bias_again(acc[272:288, :])]
    kept = pick(acc, [zl * FEAT], FEAT) + rest
    split(keep_ref, send_ref, buffer, sem, kept, pick(acc, [(1 - zl) * FEAT], FEAT) + rest)


def first_v_kernel(place_ref, own, got, v0, v1, v2, v3, acc, b1, b2, b3, sems):
    acc[...] = own[...].astype(F32) + got[...].astype(F32)
    _, _, _, y, _ = coords(place_ref)
    gap = [jnp.zeros((8, LAT), F32)]
    copies = []
    for s, buffer, out in ((1, b1, v1), (2, b2, v2), (3, b3, v3)):
        block = pick(acc, [lax.rem(y + s, 4) * FEAT], FEAT)
        buffer[...] = jnp.concatenate(block + gap, axis=0).astype(BF)
        copy = pltpu.make_async_copy(buffer, out, sems.at[s])
        copy.start()
        copies.append(copy)
    v0[...] = jnp.concatenate(pick(acc, [y * FEAT], FEAT) + gap, axis=0)
    for copy in copies:
        copy.wait()


def pick(ref, starts, rows):
    return [ref[pl.ds(pl.multiple_of(start, 8), rows), :] for start in starts]


def split(keep_ref, send_ref, buffer, sem, kept, sent):
    buffer[...] = jnp.concatenate(sent, axis=0).astype(BF)
    copy = pltpu.make_async_copy(buffer, send_ref, sem.at[0])
    copy.start()
    keep_ref[...] = jnp.concatenate(kept, axis=0)
    copy.wait()


def second_sum_kernel(
    place_ref, u_keep, u_got, v0, v1, v2, v3, _, keep_ref, send_ref, flip, buffer, sem
):
    u = u_keep[...] + u_got[...].astype(F32)
    v = (v0[...] + v1[...].astype(F32)) + (v2[...].astype(F32) + v3[...].astype(F32))
    bias = bias_again(u[144:160, :])
    stacked = jnp.concatenate(
        [u[0:128], v[0:128], u[128:136], v[128:136], jnp.zeros((112, LAT), F32)], axis=0
    )
    flip[...] = stacked.T
    zh, x, _, _, _ = coords(place_ref)

    def rows_of(dest):
        order = (x, 3 - x, jnp.bitwise_xor(x, 1), jnp.bitwise_xor(x, 2))
        return pick(flip, [(dest * 4 + dest_x) * LATP for dest_x in order], LATP)

    kept = rows_of(zh) + rows_of(3 - zh) + [bias]
    sent = rows_of(jnp.bitwise_xor(zh, 1)) + rows_of(jnp.bitwise_xor(zh, 2)) + [bias]
    split(keep_ref, send_ref, buffer, sem, kept, sent)


def third_sum_kernel(_, keep, got, keep_ref, send_ref, acc, buffer, sem):
    acc[...] = keep[...] + got[...].astype(F32)
    bias = bias_again(acc[192:208, :])
    kept = [acc[0:48, :], acc[96:144, :], bias]
    split(keep_ref, send_ref, buffer, sem, kept, [acc[48:96, :], acc[144:192, :], bias])


def fourth_sum_kernel(_, keep, got, keep_ref, send_ref, acc, buffer, sem):
    acc[...] = keep[...] + got[...].astype(F32)
    bias = bias_again(acc[96:112, :])
    kept = [acc[0:24, :], acc[48:72, :], bias]
    split(keep_ref, send_ref, buffer, sem, kept, [acc[24:48, :], acc[72:96, :], bias])


def fifth_sum_kernel(_, keep, got, keep_ref, send_ref, acc, buffer, sem):
    acc[...] = keep[...] + got[...].astype(F32)
    bias = bias_again(acc[48:64, :])
    gap = jnp.zeros((8, LAT), F32)
    split(keep_ref, send_ref, buffer, sem, [acc[0:24, :], gap, bias], [acc[24:48, :], gap, bias])


def last_kernel(keep, got, u_ref, v_ref, bias_ref):
    total = keep[...] + got[...].astype(F32)
    total = total * SCALE
    u_ref[:, 0:128] = total[0:LATP, 0:128]
    u_ref[:, 128:136] = total[0:LATP, 256:264]
    v_ref[:, 0:128] = total[0:LATP, 128:256]
    v_ref[:, 128:136] = total[0:LATP, 264:272]
    bias = total[32:38, :] + total[38:44, :]
    for j in range(D0 // 128):
        k, at = j // 3, (j % 3) * 128
        bias_ref[j : j + 1, :] = bias[k : k + 1, at : at + 128]


def index_kernel(uniq_ref, slot_ref, _, found_ref, pos_ref):
    uniq = uniq_ref[...]
    keeper = lax.shift_right_logical(uniq, 9)
    row = jnp.bitwise_and(uniq, KEEP - 1)
    upper = (
        lax.broadcasted_iota(jnp.int32, (128, 128), 0) <= lax.broadcasted_iota(jnp.int32, (128, 128), 1)
    ).astype(F32).astype(BF)
    which = lax.broadcasted_iota(jnp.int32, (N_REP, 128), 0)
    blocks = [keeper[:, b * 128 : (b + 1) * 128] for b in range(UNIQ // 128)]
    members = [(which == own).astype(F32) for own in blocks]
    running = nn(jnp.concatenate(members, axis=0).astype(BF), upper)
    carry = jnp.zeros((N_REP, 1), F32)
    ranks, keepers = [], [own.astype(F32) for own in blocks]
    for b, member in enumerate(members):
        inside = running[b * N_REP : (b + 1) * N_REP, :]
        ranks.append(jnp.sum(member * (inside + (carry - 1.0)), axis=0, keepdims=True))
        carry = carry + inside[:, 127:128]
    member = jnp.concatenate(members, axis=1)
    rank = jnp.concatenate(ranks, axis=1)
    row_high = lax.shift_right_logical(row, 8).astype(F32)
    row_low = jnp.bitwise_and(row, 255).astype(F32)
    digits = jnp.concatenate([member * row_high, member * row_low], axis=0).astype(BF)
    ranked = lax.broadcasted_iota(jnp.int32, (CAP, UNIQ), 0).astype(F32) == rank
    where = nt(digits, ranked.astype(F32).astype(BF))
    wide = jnp.concatenate([where, jnp.zeros((2 * N_REP, 256 - CAP), F32)], axis=1)
    for k in range(N_REP):
        high, low = wide[k : k + 1, :], wide[N_REP + k : N_REP + k + 1, :]
        block = [high[:, 0:128], high[:, 128:256], low[:, 0:128], low[:, 128:256]]
        pos_ref[k] = jnp.concatenate(block + [jnp.zeros((12, 128), F32)], axis=0).astype(BF)
    table = jnp.concatenate(ranks + keepers, axis=0).astype(BF)
    found = []
    for p in range(2):
        slot = slot_ref[p : p + 1, :]
        low = jnp.bitwise_and(slot, 127)
        high = lax.shift_right_logical(slot, 7)
        hot_low = (lax.broadcasted_iota(jnp.int32, (128, SAMP), 0) == low).astype(F32).astype(BF)
        picked = nn(table, hot_low)
        hot_high = (lax.broadcasted_iota(jnp.int32, (16, SAMP), 0) == high).astype(F32)
        found.append(
            (
                jnp.sum(hot_high * picked[0:16, :], axis=0, keepdims=True),
                jnp.sum(hot_high * picked[16:32, :], axis=0, keepdims=True),
            )
        )
    rows = [row for pair in found for row in pair]
    found_ref[...] = jnp.concatenate(rows + [jnp.zeros((4, SAMP), F32)], axis=0)


def rows_kernel(found_ref, got_ref, pos_ref, _, out_hbm, hot, out_ref, sems):
    places = lax.broadcasted_iota(jnp.int32, (CAP, SAMP), 0).astype(F32).astype(BF)
    one, zero = jnp.ones((CAP, SAMP), BF), jnp.zeros((CAP, SAMP), BF)
    stores = []
    for j in range(2):
        for i in range(8):
            k = j * 8 + i
            hits = []
            for p in range(2):
                at, kept = found_ref[2 * p : 2 * p + 1, :], found_ref[2 * p + 1 : 2 * p + 2, :]
                own = jnp.where(kept == float(k), at, -1.0).astype(BF)
                hits.append(jnp.where(places == own, one, zero))
            hot[j % 2, i * CAP : (i + 1) * CAP, :] = hits[0] + hits[1]
        sums = nn(hot[j % 2], got_ref[...])
        for i in range(0, 8, 2):
            pair = []
            for k in (i, i + 1):
                pair += [sums[k * CAP : (k + 1) * CAP, :], pos_ref[j * 8 + k].astype(F32)[0:8, :]]
            start = (j * 8 + i) * PAYLOAD
            out_ref[start : start + 2 * PAYLOAD, :] = jnp.concatenate(pair, axis=0).astype(BF)
        some = slice(j * 8 * PAYLOAD, (j + 1) * 8 * PAYLOAD)
        store = pltpu.make_async_copy(out_ref.at[some], out_hbm.at[some], sems.at[j])
        store.start()
        stores.append(store)
    for store in stores:
        store.wait()


def keep_kernel(got_ref, out_ref):
    wide = N_REP * PAYLOAD
    nowhere = jnp.full((1, PAYLOAD - CAP), -1.0, F32)
    digits = []
    for i in (0, 2):
        pieces = []
        for g in range(N_REP):
            start = g * PAYLOAD + CAP - 8 * (g % 2)
            pos = got_ref[start : start + 16, :].astype(F32)[8 * (g % 2) : 8 * (g % 2) + 8, :]
            pieces += [pos[i : i + 1, :], pos[i + 1 : i + 2, 0 : CAP - 128], nowhere]
        digits.append(jnp.concatenate(pieces, axis=1))
    got = got_ref[...]
    names = lax.broadcasted_iota(jnp.int32, (256, wide), 0).astype(F32).astype(BF)
    one, zero = jnp.ones((256, wide), BF), jnp.zeros((256, wide), BF)
    for half in range(2):
        own = jnp.where(digits[0] == float(half), digits[1], -1.0).astype(BF)
        out_ref[half * 256 : (half + 1) * 256, :] = nn(jnp.where(names == own, one, zero), got)


def call(kernel, outs, ins, scratch=(), mib=24, spare=None, us=2):
    return pl.pallas_call(
        kernel,
        out_shape=tuple(jax.ShapeDtypeStruct(s, d) for _, s, d in outs),
        in_specs=[spec for spec, _ in ins],
        out_specs=tuple(spec for spec, _, _ in outs),
        scratch_shapes=list(scratch),
        input_output_aliases={} if spare is None else {spare[0]: spare[1]},
        compiler_params=params(mib),
        cost_estimate=pl.CostEstimate(flops=us * 10**9, bytes_accessed=us * 10**6, transcendentals=0),
    )(*[a for _, a in ins])


def near(*arrays):
    return [(VMEM, a) for a in arrays]


def shifted(messages, axis):
    got = {
        s: lax.ppermute(messages[s - 1], axis, [(i, (i + s) % 4) for i in range(4)]) for s in (2, 1, 3)
    }
    return [got[s] for s in (1, 2, 3)]


def shards(dense, pooled, cot, proj_v, proj_u, bias, lookup_slot, uniq_rows):
    place = (SMEM, lax.axis_index(REP + TABLE).astype(jnp.int32).reshape(1))
    swap = [(0, 1), (1, 0)]
    other = [lax.ppermute(a, "c", swap) for a in (dense, pooled, cot)]
    dma = pltpu.SemaphoreType.DMA
    dense2, pooled2, cot2 = other
    u_shape, v_shape = (288, LAT), (544, LAT)
    bias_rows, out_shape = (D0 // 128, 128), (N_TAB, 128, EMB)
    loaded = (pooled, pooled2, dense, dense2, proj_v, cot, cot2, proj_u, bias.reshape(bias_rows))
    u0, u1, u2, u3, v_keep, v_send, outgoing = call(
        weight_kernel,
        [(HBM, u_shape, BF)] * 4 + [(HBM, v_shape, BF)] * 2 + [(HBM, out_shape, BF)],
        [place] + [(HBM, a) for a in loaded],
        [pltpu.VMEM((256, w), BF) for w in (D0 - EMB, EMB, D0, D0)]
        + [pltpu.VMEM((D0, LAT), BF), pltpu.VMEM((LAT, D0), BF)]
        + [pltpu.VMEM((D0, LAT), F32), pltpu.VMEM((D0, LAT), F32), pltpu.VMEM((1, D0), F32)]
        + [pltpu.VMEM(u_shape, BF)] * 4
        + [pltpu.VMEM(v_shape, BF)] * 2
        + [pltpu.VMEM(bias_rows, F32), pltpu.VMEM(out_shape, BF)]
        + [dma((9,)), dma((6,)), dma((4,))],
        mib=56,
        us=8,
    )
    received = lax.all_to_all(outgoing, TABLE, 0, 0, tiled=True).reshape(SAMP, EMB)
    u_got = shifted([u1, u2, u3], "y")
    v_got = lax.ppermute(v_send, "zl", swap)
    u_shape, v_shape = (160, LAT), (144, LAT)
    v0, v1, v2, v3 = call(
        first_v_kernel,
        [(VMEM, v_shape, F32)] + [(HBM, v_shape, BF)] * 3,
        [place] + near(v_keep, v_got),
        [pltpu.VMEM((544, LAT), F32)] + [pltpu.VMEM(v_shape, BF)] * 3 + [dma((4,))],
        us=2,
    )
    v_got = shifted([v1, v2, v3], "y")
    u_keep, u_send = call(
        first_u_kernel,
        [(VMEM, u_shape, F32), (HBM, u_shape, BF)],
        [place] + near(u0, *u_got) + [(ANY, v0)],
        [pltpu.VMEM((288, LAT), F32), pltpu.VMEM(u_shape, BF), dma((1,))],
        us=100,
    )
    found, pos = call(
        index_kernel,
        [(VMEM, (8, SAMP), F32), (VMEM, (N_REP, 16, 128), BF)],
        near(uniq_rows.reshape(1, UNIQ), lookup_slot.reshape(SAMP, 2).T) + [(ANY, u_keep)],
        mib=24,
    )
    (payload,) = call(
        rows_kernel,
        [(HBM, (N_REP * PAYLOAD, EMB), BF)],
        near(found, received, pos) + [(ANY, u_keep)],
        [pltpu.VMEM((2, 8 * CAP, SAMP), BF), pltpu.VMEM((N_REP * PAYLOAD, EMB), BF), dma((2,))],
        us=7,
    )
    u_got = lax.ppermute(u_send, "zl", swap)
    flat = [(0, 1), (1, 0), (2, 3), (3, 2)]
    cross = [(0, 3), (3, 0), (1, 2), (2, 1)]

    def halve(kernel, ins, in_rows, rows, axis, pairs, us=2, after=()):
        kept, sent = call(
            kernel,
            [(VMEM, (rows, LAT), F32), (HBM, (rows, LAT), BF)],
            [place] + near(*ins) + [(ANY, a) for a in after],
            [pltpu.VMEM((in_rows, LAT), F32), pltpu.VMEM((rows, LAT), BF), dma((1,))],
            us=us,
        )
        return kept, lax.ppermute(sent, axis, pairs)

    both = halve(second_sum_kernel, (u_keep, u_got, v0, *v_got), LAT, 208, "zh", flat, after=(payload,))
    gathered = lax.all_to_all(payload, REP, 0, 0, tiled=True)
    both = halve(third_sum_kernel, both, 208, 112, "x", flat, us=100)
    both = halve(fourth_sum_kernel, both, 112, 64, "x", cross)
    both = halve(fifth_sum_kernel, both, 64, 48, "zh", cross)
    part_u, part_v, whole_bias = call(
        last_kernel,
        [(VMEM, (LATP, FEAT), F32), (VMEM, (LATP, FEAT), F32), (VMEM, (D0 // 128, 128), F32)],
        near(*both),
    )
    (row_part,) = call(keep_kernel, [(VMEM, (KEEP, EMB), F32)], near(gathered))
    return part_u, part_v.T, whole_bias.reshape(D0), row_part.reshape(1, KEEP, EMB)


def solution(mesh):
    fine = Mesh(np.asarray(mesh.devices).reshape(4, 4, 2, 4, 2), ("zh", "x", "zl", "y", "c"))
    every = P(REP + TABLE, None)
    placed = (every, every, every, P(), P(), P(), P(REP, TABLE, None), P(REP, TABLE, None))
    return jax.shard_map(
        shards,
        mesh=fine,
        in_specs=placed,
        out_specs=(P(REP, TABLE), P(TABLE, REP), P(), P(TABLE, REP, None)),
        check_vma=False,
    )
```
